768 devices in a mesh: dp: 96 (over y, z), expert: 8 (over x, core).
Axes of the slice: x: 4, y: 8, z: 12, core: 2. Of those that a mesh axis runs over, the one named last changes fastest.
Arguments:
- tokens: bfloat16 [12288, 3584], P('dp', 'expert'), may hold values from -6 to 6
- cotangent: bfloat16 [12288, 3584], P('dp', 'expert'), may hold values from -6 to 6
- slot_route: int32 [12288, 2], P('dp'), may hold values from 0 to 191, all different within a row; in each aligned block of 128 rows (0 to 127, 128 to 255, ...) at most 2 rows name the same one
- route_weight: float32 [12288, 2], P('dp'), may hold values from 0.1 to 1
- w_gate: bfloat16 [96, 3584, 1024], P('dp', 'expert'), may hold values from -0.09375 to 0.09375
- w_down: bfloat16 [96, 1024, 3584], P('dp', None, 'expert'), may hold values from -0.1875 to 0.1875
Outputs:
- mixed: bfloat16 [12288, 3584], P('dp', 'expert')
- input_grad: bfloat16 [12288, 3584], P('dp', 'expert')
- gate_grad: bfloat16 [96, 3584, 1024], P('dp', 'expert')
- down_grad: bfloat16 [96, 1024, 3584], P('dp', None, 'expert')
The draws below stay inside these ranges and needn't reach their ends.
Inputs may be any that keep to these rules, and one draw needn't show every extreme that they name: `slot_route`: in each group of 128 tokens no slot is named by more than 2 picks, a bound that some block reaches; a token names 2 different slots.
All inputs are finite; a program needn't handle non-finite values.
Results may differ from the reference program's by a relative error of at most 0.024.
Values may be sent and summed in bfloat16 or wider, within the bound.
A program may use at most 32 MiB of HBM per device.

```python
import math
import jax
import jax.numpy as jnp
import numpy as np
from jax import lax

D = 3584
HW = 1024
TOPK = 2
TOK_DEV = 128
EXPERTS = 96
TOKENS = 12288
CAP = 2
N_DP = 96
N_EXPERT = 8


def level_of(stream_key, extent, cuts, low, largest):
    def one(dim, blocks):
        draws = jax.random.uniform(jax.random.fold_in(jax.random.fold_in(stream_key, 6), dim), (blocks,), jnp.float32, low / len(cuts), largest / len(cuts))
        return jnp.repeat(jnp.exp(draws), extent[dim] // blocks).reshape((-1,) + (1,) * (len(extent) - dim - 1))

    gain = one(*cuts[0])
    for cut in cuts[1:]:
        gain = gain * one(*cut)
    return gain


def shared_out(stream_key, own, number, rows, count, top, most, skew):
    sequence = jax.random.permutation(stream_key, count)
    heavy_load, common = load_shares(count, rows * top, most, skew, True), load_shares(count, rows * top, most, skew, False)
    places = jnp.arange(count)

    def named(tallies, rotation):
        used = int((tallies > 0).sum())
        fixed = max(1, used // 4)
        passed = fixed + (places - fixed + rotation * (used - fixed)) % max(1, count - fixed)
        return jnp.zeros((count,), jnp.int32).at[sequence[jnp.where(places < fixed, places, passed)]].set(jnp.asarray(tallies, jnp.int32))

    tallies = jnp.where(number % 4 == 0, named(heavy_load, number // 4), named(common, number - number // 4 - 1))
    mixed = jax.random.permutation(jax.random.fold_in(own, 3), count)
    source_of, receiver = mixed[0:count // 2 * 2:2], mixed[1:count // 2 * 2:2]
    margin = jnp.minimum(tallies[source_of] - 1, most - tallies[receiver]) // 2
    margin = jnp.where((source_of == sequence[0]) | (receiver == sequence[0]) | (tallies[receiver] == 0), 0, jnp.maximum(margin, 0))
    passed = jax.random.randint(jax.random.fold_in(own, 4), (count // 2,), 0, 1 << 20) % (margin + 1)
    tallies = tallies.at[source_of].add(-passed).at[receiver].add(passed)
    labels = jnp.searchsorted(jnp.cumsum(tallies), jnp.arange(rows * top), side="right").astype(jnp.int32)
    listing = labels.reshape(top, rows).T
    listing = listing[jax.random.permutation(jax.random.fold_in(own, 1), rows)]
    rotation = jax.random.randint(jax.random.fold_in(own, 2), (rows, 1), 0, top)
    return jnp.take_along_axis(listing, (jnp.arange(top)[None, :] + rotation) % top, axis=1)


def load_shares(number_of, total, bound, lean, full):
    portions = [(1 << 20) // math.isqrt(rank ** lean) + 1 for rank in range(1, number_of + 1)]
    largest = bound if full else min(bound, max(-(-total // number_of), total * portions[0] // sum(portions)))
    least = 1 if total - largest >= number_of - 1 else 0
    counts, rest = [largest] + [least] * (number_of - 1), total - largest - least * (number_of - 1)
    while rest > 0:
        movable = [i for i in range(1, number_of) if counts[i] < largest] or [i for i in range(1, number_of) if counts[i] < bound]
        mass, left = sum([portions[i] for i in movable]), rest
        for i in movable:
            extra = min(bound - counts[i], max(1, left * portions[i] // mass), rest)
            counts[i] = counts[i] + extra
            rest = rest - extra
    return np.array(counts)


def centred(rng, shape, spread, limit, split=(), kind=jnp.bfloat16):
    result = jax.random.normal(rng, shape, jnp.float32) * spread
    if len(split) > 0:
        result = level_of(rng, shape, split, -0.22, 0.18) * result
    return jnp.clip(result, min=-limit, max=limit).astype(kind)


def setup_inputs(seed: int = 0) -> dict:
    streams_of = jax.random.split(jax.random.key(seed), 7)
    tokens = centred(streams_of[0], (TOKENS, D), 1.0, 6.0, ((0, 96), (1, 8)))
    cotangent = centred(streams_of[1], (TOKENS, D), 1.0, 6.0, ((0, 96), (1, 8)))
    slot_route_keys = jax.random.split(jax.random.fold_in(streams_of[2], 1), TOKENS // TOK_DEV)
    slot_route_turns = jax.random.permutation(jax.random.fold_in(streams_of[2], 3), TOKENS // TOK_DEV)
    slot_route = jax.vmap(lambda own, number: shared_out(jax.random.fold_in(streams_of[2], 2), own, number, TOK_DEV, 2 * N_DP, TOPK, CAP, 2))(slot_route_keys, slot_route_turns).reshape((TOKENS, TOPK))
    route_weight = jnp.clip(jnp.exp(math.log(1.0) - 2.3025851 * jax.random.uniform(streams_of[3], (TOKENS, TOPK), jnp.float32) ** level_of(streams_of[3], (TOKENS, TOPK), ((0, 96),), -0.2, 0.2)), 0.1, 1.0)
    w_gate = centred(streams_of[4], (EXPERTS, D, HW), D ** -0.5, 0.09375, ((0, 96), (1, 8)))
    w_down = centred(streams_of[5], (EXPERTS, HW, D), HW ** -0.5, 0.1875, ((0, 96), (2, 8)))
    return {"tokens": tokens, "cotangent": cotangent, "slot_route": slot_route, "route_weight": route_weight, "w_gate": w_gate, "w_down": w_down}


def block_sum(operand, weight_blocks):
    pieces = jnp.einsum('mfd,fdh->mfh', operand, weight_blocks.astype(jnp.float32))
    pieces = lax.optimization_barrier(pieces.astype(jnp.bfloat16))
    return jnp.sum(pieces.astype(jnp.float32), axis=1)


def slot_math(gate_mat, down_mat, slot_rows, slot_scaled):
    row_count = slot_rows.shape[0]
    width_part = D // N_EXPERT
    operand = slot_rows.reshape(row_count, N_EXPERT, width_part).astype(jnp.float32)
    gate_vals = block_sum(operand, gate_mat.reshape(N_EXPERT, width_part, HW))
    sig_gate = jax.nn.sigmoid(gate_vals)
    hidden = (gate_vals * sig_gate).astype(jnp.bfloat16)
    slot_out = jnp.dot(hidden, down_mat, preferred_element_type=jnp.float32).astype(jnp.bfloat16)
    scaled_blocks = slot_scaled.reshape(row_count, N_EXPERT, width_part).astype(jnp.float32)
    down_blocks = jnp.transpose(down_mat.reshape(HW, N_EXPERT, width_part), (1, 2, 0))
    grad_hidden = block_sum(scaled_blocks, down_blocks)
    grad_gate = (grad_hidden * sig_gate * (1.0 + gate_vals * (1.0 - sig_gate))).astype(jnp.bfloat16)
    slot_dx = jnp.dot(grad_gate, gate_mat.T, preferred_element_type=jnp.float32).astype(jnp.bfloat16)
    gate_part = jnp.dot(slot_rows.T, grad_gate, preferred_element_type=jnp.float32).astype(jnp.bfloat16)
    down_part = jnp.dot(hidden.T, slot_scaled, preferred_element_type=jnp.float32).astype(jnp.bfloat16)
    return slot_out, slot_dx, gate_part, down_part


def add_pair(first, second):
    first = lax.optimization_barrier(first)
    second = lax.optimization_barrier(second)
    return (first.astype(jnp.float32) + second.astype(jnp.float32)).astype(jnp.bfloat16)


def reference(tokens, cotangent, slot_route, route_weight, w_gate, w_down):
    n_slots = 2 * EXPERTS
    half_dp = EXPERTS // 2
    slot_len = N_DP * CAP
    grouped = slot_route.reshape(N_DP, TOK_DEV * TOPK)
    onehot = (grouped[:, :, None] == jnp.arange(n_slots, dtype=jnp.int32)[None, None, :]).astype(jnp.int32)
    position = jnp.sum((jnp.cumsum(onehot, axis=1) - onehot) * onehot, axis=2).astype(jnp.int32)
    slot_row = (jnp.arange(N_DP, dtype=jnp.int32)[:, None] * CAP + position).astype(jnp.int32)
    picks_all = jnp.arange(N_DP * TOK_DEV * TOPK, dtype=jnp.int32).reshape(N_DP, TOK_DEV * TOPK)
    table = jnp.full((n_slots, slot_len), -1, jnp.int32).at[grouped, slot_row].set(picks_all)
    scaled_all = (route_weight[:, :, None] * cotangent[:, None, :].astype(jnp.float32)).astype(jnp.bfloat16)
    scaled_all = scaled_all.reshape(TOKENS * TOPK, D)

    def rows_of(slot):
        entries = table[slot]
        filled = (entries >= 0)[:, None]
        safe = jnp.maximum(entries, 0).astype(jnp.int32)
        slot_rows = jnp.where(filled, tokens[safe // TOPK], jnp.zeros((), jnp.bfloat16)).astype(jnp.bfloat16)
        slot_scaled = jnp.where(filled, scaled_all[safe], jnp.zeros((), jnp.bfloat16)).astype(jnp.bfloat16)
        return slot_rows, slot_scaled

    def one_expert(expert):
        home = (2 * expert).astype(jnp.int32)
        copy_slot = (2 * ((expert + half_dp) % EXPERTS) + 1).astype(jnp.int32)
        home_rows, home_scaled = rows_of(home)
        copy_rows, copy_scaled = rows_of(copy_slot)
        home_out = slot_math(w_gate[expert], w_down[expert], home_rows, home_scaled)
        copy_out = slot_math(w_gate[expert], w_down[expert], copy_rows, copy_scaled)
        return (home_out[0], home_out[1], copy_out[0], copy_out[1],
                add_pair(home_out[2], copy_out[2]), add_pair(home_out[3], copy_out[3]))

    results = lax.map(one_expert, jnp.arange(EXPERTS, dtype=jnp.int32))
    home_y, home_dx, copy_y, copy_dx, gate_grad, down_grad = results
    slots_y = jnp.stack([home_y, jnp.roll(copy_y, half_dp, axis=0)], axis=1).reshape(n_slots, slot_len, D)
    slots_dx = jnp.stack([home_dx, jnp.roll(copy_dx, half_dp, axis=0)], axis=1).reshape(n_slots, slot_len, D)
    flat_slots = grouped.reshape(-1)
    flat_rows = slot_row.reshape(-1)
    picked_y = slots_y[flat_slots, flat_rows].astype(jnp.float32).reshape(TOKENS, TOPK, D)
    picked_dx = slots_dx[flat_slots, flat_rows].astype(jnp.float32).reshape(TOKENS, TOPK, D)
    mixed = jnp.sum(route_weight[:, :, None] * picked_y, axis=1).astype(jnp.bfloat16)
    input_grad = jnp.sum(picked_dx, axis=1).astype(jnp.bfloat16)
    return mixed, input_grad, gate_grad, down_grad
```

```python
import jax
import jax.numpy as jnp
from jax import lax
from jax.sharding import PartitionSpec as P


def move_rows(tensors):
    return (
        lax.all_to_all(tensors[0], "dp", split_axis=0, concat_axis=0, tiled=True),
        lax.all_to_all(tensors[1], "dp", split_axis=0, concat_axis=0, tiled=True),
    )


def reduce_hidden(partials):
    return lax.psum(partials.astype(jnp.bfloat16), "expert").astype(jnp.float32)


def project(operand, weight, pattern_each):
    return jnp.einsum(pattern_each, operand, weight, preferred_element_type=jnp.float32)


def expert_pass(weights, slot_rows, slot_scaled):
    gate_mat, down_mat = weights
    gate_part = project(slot_rows, gate_mat, "md,dh->mh")
    gate_vals = reduce_hidden(gate_part)
    sig_gate = jax.nn.sigmoid(gate_vals)
    hidden_local = (gate_vals * sig_gate).astype(jnp.bfloat16)
    hidden = hidden_local
    slot_out = project(hidden, down_mat, "mh,hd->md").astype(jnp.bfloat16)
    hidden_part = project(slot_scaled, down_mat, "md,hd->mh")
    grad_hidden = reduce_hidden(hidden_part)
    grad_gate = (grad_hidden * sig_gate * (1.0 + gate_vals * (1.0 - sig_gate))).astype(jnp.bfloat16)
    gate_full = grad_gate
    slot_dx = project(gate_full, gate_mat, "mh,dh->md").astype(jnp.bfloat16)
    gate_part_grad = jnp.einsum(
        "md,mh->dh", slot_rows, gate_full, preferred_element_type=jnp.float32
    ).astype(jnp.bfloat16)
    down_part_grad = jnp.einsum(
        "mh,md->hd", hidden, slot_scaled, preferred_element_type=jnp.float32
    ).astype(jnp.bfloat16)
    return (slot_out, slot_dx, gate_part_grad, down_part_grad)


def per_device(tokens, cotangent, slot_route, route_weight, w_gate, w_down):
    n_dp = lax.axis_size("dp")
    half_dp = n_dp // 2
    n_slots = 2 * n_dp
    tok_rows, width = tokens.shape
    picks = slot_route.shape[1]
    capacity = max(2, tok_rows * picks * 3 // (4 * n_dp))
    flat_slots = slot_route.reshape(-1)
    onehot = (flat_slots[:, None] == jnp.arange(n_slots, dtype=jnp.int32)[None, :]).astype(
        jnp.int32
    )
    position = jnp.sum((jnp.cumsum(onehot, axis=0) - onehot) * onehot, axis=1)
    pair = flat_slots // 2
    odd = flat_slots % 2
    home = jnp.where(odd == 1, (pair + half_dp) % n_dp, pair)
    target = (home * 2 + odd) * capacity + position
    sources = jnp.repeat(tokens, picks, axis=0)
    scaled = (
        route_weight.reshape(-1, 1) * jnp.repeat(cotangent, picks, axis=0).astype(jnp.float32)
    ).astype(jnp.bfloat16)
    empty = jnp.zeros((n_slots * capacity, width), jnp.bfloat16)
    send_rows = empty.at[target].set(sources).reshape(n_dp, 2 * capacity, width)
    send_scaled = empty.at[target].set(scaled).reshape(n_dp, 2 * capacity, width)
    got_rows, got_scaled = move_rows((send_rows, send_scaled))
    results = expert_pass(
        (w_gate[0], w_down[0]), got_rows.reshape(-1, width), got_scaled.reshape(-1, width)
    )
    slot_out, slot_dx, gate_grad, down_grad = results
    back_out, back_dx = move_rows(
        (
            slot_out.reshape(n_dp, 2 * capacity, width),
            slot_dx.reshape(n_dp, 2 * capacity, width),
        )
    )
    picked_out = (
        back_out.reshape(-1, width)[target].astype(jnp.float32).reshape(tok_rows, picks, width)
    )
    picked_dx = (
        back_dx.reshape(-1, width)[target].astype(jnp.float32).reshape(tok_rows, picks, width)
    )
    mixed = jnp.sum(route_weight[:, :, None] * picked_out, axis=1).astype(jnp.bfloat16)
    input_grad = jnp.sum(picked_dx, axis=1).astype(jnp.bfloat16)
    return (mixed, input_grad, gate_grad[None], down_grad[None])


def solution(mesh):
    return jax.shard_map(
        per_device,
        mesh=mesh,
        in_specs=(
            P("dp", "expert"),
            P("dp", "expert"),
            P("dp", None),
            P("dp", None),
            P("dp", "expert", None),
            P("dp", None, "expert"),
        ),
        out_specs=(
            P("dp", "expert"),
            P("dp", "expert"),
            P("dp", "expert", None),
            P("dp", None, "expert"),
        ),
        check_vma=False,
    )
```

```python
import jax
import jax.numpy as jnp
from jax import lax
from jax.experimental import pallas as pl
from jax.experimental.pallas import tpu as pltpu
from jax.sharding import PartitionSpec as P

NY, NZ, NX, NCORE = 8, 12, 4, 2
BF16, F32 = jnp.bfloat16, jnp.float32
TOK = 128
WIDTH = 448
LANES = 2 * WIDTH
ROWS = 2 * NY * NZ
HW = 1024
PART = ROWS // NX
PAD = 64
TILE = 512


def spread(k, n):
    return n // 2 + (k // 2) * (1 - 2 * (k % 2))


def dot(a, b, contract_a=1, contract_b=0):
    return lax.dot_general(a, b, (((contract_a,), (contract_b,)), ((), ())), preferred_element_type=F32)


def layer(
    tok_hbm, cot_hbm, slot_ref, weight_ref, gate_hbm, down_hbm,
    mixed_ref, grad_ref, gate_grad_hbm, down_grad_hbm,
    tok_src, cot_src, gate_w, down_w, pick, perm_out, perm_back,
    z_out, z_in, y_out, y_in, rows,
    core_out, core_in, own, x_out, x_in, hid, gate_keep,
    yb_out, yb_in, zb_out, zb_in, grad_w,
    load_sem, store_sem,
    z_send, z_recv, y_send, y_recv, c_send, c_recv, x_send, x_recv,
    g_send, g_recv, f_send, f_recv, yb_send, yb_recv, zb_send, zb_recv,
):
    dp, ex = lax.axis_index("dp"), lax.axis_index("expert")
    y, z = dp // NZ, dp % NZ
    x, core = ex // NCORE, ex % NCORE
    other = 1 - core

    def at_z(k):
        return (y * NZ + (z + spread(k, NZ)) % NZ, ex)

    def at_y(k):
        return (((y + spread(k, NY)) % NY) * NZ + z, ex)

    def at_x(k):
        return (dp, ((x + spread(k, NX)) % NX) * NCORE + core)

    at_core = (dp, x * NCORE + other)

    loads = [
        pltpu.make_async_copy(tok_hbm, tok_src.at[pl.ds(0, WIDTH), pl.ds(0, TOK)], load_sem.at[0]),
        pltpu.make_async_copy(tok_hbm, tok_src.at[pl.ds(WIDTH, WIDTH), pl.ds(TOK, TOK)], load_sem.at[1]),
        pltpu.make_async_copy(cot_hbm, cot_src.at[pl.ds(0, WIDTH), pl.ds(0, TOK)], load_sem.at[2]),
        pltpu.make_async_copy(cot_hbm, cot_src.at[pl.ds(WIDTH, WIDTH), pl.ds(TOK, TOK)], load_sem.at[3]),
        pltpu.make_async_copy(gate_hbm, gate_w.at[pl.ds(PAD, WIDTH)], load_sem.at[4]),
        pltpu.make_async_copy(down_hbm, down_w.at[pl.ds(PAD, WIDTH)], load_sem.at[5]),
    ]
    for load in loads:
        load.start()

    barrier = pltpu.get_barrier_semaphore()

    def hello(place, count):
        def one(k, carry):
            pl.semaphore_signal(barrier, inc=1, device_id=place(k), device_id_type=pl.DeviceIdType.MESH)
            return carry

        lax.fori_loop(1, count, one, 0)

    hello(at_z, NZ)
    hello(at_y, NY)
    hello(at_x, NX)
    pl.semaphore_signal(barrier, inc=1, device_id=at_core, device_id_type=pl.DeviceIdType.MESH)

    j = lax.broadcasted_iota(jnp.int32, (ROWS, TOK), 0)
    to = ((j >> 1) & (NY - 1)) * NZ + (j >> 4)
    half = NY * NZ // 2
    slot = jnp.where((j & 1) == 1, 2 * jnp.where(to < half, to + half, to - half) + 1, 2 * to)
    is_0, is_1 = slot == slot_ref[0:1, :], slot == slot_ref[1:2, :]
    named = jnp.where(is_0 | is_1, 1.0, 0.0)
    earlier = lax.broadcasted_iota(jnp.int32, (TOK, TOK), 0) < lax.broadcasted_iota(jnp.int32, (TOK, TOK), 1)
    before = dot(named.astype(BF16), jnp.where(earlier, 1.0, 0.0).astype(BF16))
    first = jnp.where(before < 0.5, 1.0, 0.0)
    later = 1.0 - first
    one_0, one_1 = jnp.where(is_0, 1.0, 0.0), jnp.where(is_1, 1.0, 0.0)
    pick[0] = jnp.concatenate([one_0 * first, one_1 * first], axis=1).astype(BF16)
    pick[1] = jnp.concatenate([one_0 * later, one_1 * later], axis=1).astype(BF16)
    chosen = jnp.concatenate([named * first, named * later], axis=1).astype(BF16)
    weight_of = one_0 * weight_ref[0:1, :] + one_1 * weight_ref[1:2, :]
    scale_first = jnp.sum(weight_of * first, axis=1, keepdims=True)
    scale_later = jnp.sum(weight_of * later, axis=1, keepdims=True)
    lane = lax.broadcasted_iota(jnp.int32, (ROWS, LANES), 1)
    scale = jnp.where(lane < WIDTH, scale_first, scale_later)

    down_axis = lax.broadcasted_iota(jnp.int32, (ROWS, ROWS), 0)
    along_axis = lax.broadcasted_iota(jnp.int32, (ROWS, ROWS), 1)

    def place(c):
        return ((c >> 1) & (NY - 1)) * (2 * NZ) + (c >> 4) * 2 + (c & 1)

    perm_out[...] = jnp.where(down_axis == place(along_axis), 1.0, 0.0).astype(BF16)
    perm_back[...] = jnp.where(place(down_axis) == along_axis, 1.0, 0.0).astype(BF16)

    for src in (tok_src, cot_src):
        src[pl.ds(0, WIDTH), pl.ds(TOK, TOK)] = jnp.zeros((WIDTH, TOK), BF16)
        src[pl.ds(WIDTH, WIDTH), pl.ds(0, TOK)] = jnp.zeros((WIDTH, TOK), BF16)
    for mat in (gate_w, down_w):
        mat[pl.ds(0, PAD), :] = jnp.zeros((PAD, HW), BF16)
        mat[pl.ds(PAD + WIDTH, PAD), :] = jnp.zeros((PAD, HW), BF16)

    def z_copy(src, dst, send, recv, a, k):
        off = spread(k, NZ)
        return pltpu.make_async_remote_copy(
            src_ref=src.at[a, (z + off) % NZ], dst_ref=dst.at[a, z], send_sem=send.at[a, off],
            recv_sem=recv.at[a, off], device_id=at_z(k), device_id_type=pl.DeviceIdType.MESH)

    def z_come(src, dst, send, recv, a, k):
        off = spread(k, NZ)
        return pltpu.make_async_remote_copy(
            src_ref=src.at[a, z], dst_ref=dst.at[a, (z + NZ - off) % NZ], send_sem=send.at[a, off],
            recv_sem=recv.at[a, off], device_id=at_z(k), device_id_type=pl.DeviceIdType.MESH)

    def y_copy(src, dst, send, recv, a, k):
        off = spread(k, NY)
        return pltpu.make_async_remote_copy(
            src_ref=src.at[a, (y + off) % NY], dst_ref=dst.at[a, y], send_sem=send.at[a, off],
            recv_sem=recv.at[a, off], device_id=at_y(k), device_id_type=pl.DeviceIdType.MESH)

    def y_come(src, dst, send, recv, a, k):
        off = spread(k, NY)
        return pltpu.make_async_remote_copy(
            src_ref=src.at[a, y], dst_ref=dst.at[a, (y + NY - off) % NY], send_sem=send.at[a, off],
            recv_sem=recv.at[a, off], device_id=at_y(k), device_id_type=pl.DeviceIdType.MESH)

    def x_copy(a, k):
        off = spread(k, NX)
        return pltpu.make_async_remote_copy(
            src_ref=x_out.at[a, (x + off) % NX], dst_ref=x_in.at[a, x], send_sem=x_send.at[a, off],
            recv_sem=x_recv.at[a, off], device_id=at_x(k), device_id_type=pl.DeviceIdType.MESH)

    def x_come(a, k):
        off = spread(k, NX)
        return pltpu.make_async_remote_copy(
            src_ref=x_out.at[a, x], dst_ref=x_in.at[a, (x + NX - off) % NX], send_sem=x_send.at[a, off],
            recv_sem=x_recv.at[a, off], device_id=at_x(k), device_id_type=pl.DeviceIdType.MESH)

    def g_copy(a, k):
        off = spread(k, NX)
        return pltpu.make_async_remote_copy(
            src_ref=hid.at[a, core, x], dst_ref=hid.at[a, core, x], send_sem=g_send.at[a, off],
            recv_sem=g_recv.at[a, off], device_id=at_x(k), device_id_type=pl.DeviceIdType.MESH)

    def g_come(a, k):
        off = spread(k, NX)
        frm = (x + NX - off) % NX
        return pltpu.make_async_remote_copy(
            src_ref=hid.at[a, core, x], dst_ref=hid.at[a, core, frm], send_sem=g_send.at[a, off],
            recv_sem=g_recv.at[a, off], device_id=at_x(k), device_id_type=pl.DeviceIdType.MESH)

    def f_copy(a, off):
        frm = (x + NX - off) % NX
        return pltpu.make_async_remote_copy(
            src_ref=hid.at[a, core, frm], dst_ref=hid.at[a, core, frm], send_sem=f_send.at[a, off],
            recv_sem=f_recv.at[a, off], device_id=at_core, device_id_type=pl.DeviceIdType.MESH)

    def f_come(a, off):
        frm = (x + NX - off) % NX
        return pltpu.make_async_remote_copy(
            src_ref=hid.at[a, core, frm], dst_ref=hid.at[a, other, frm], send_sem=f_send.at[a, off],
            recv_sem=f_recv.at[a, off], device_id=at_core, device_id_type=pl.DeviceIdType.MESH)

    def c_copy(a):
        return pltpu.make_async_remote_copy(
            src_ref=core_out.at[a], dst_ref=core_in.at[a], send_sem=c_send.at[a],
            recv_sem=c_recv.at[a], device_id=at_core, device_id_type=pl.DeviceIdType.MESH)

    def each(n, step):
        def one(k, carry):
            step(k)
            return carry

        lax.fori_loop(1, n, one, 0)

    def send_z(src, dst, send, recv, a):
        each(NZ, lambda k: z_copy(src, dst, send, recv, a, k).start())
        dst[a, z] = src[a, z]

    def take_z(src, dst, send, recv, a):
        each(NZ, lambda k: z_come(src, dst, send, recv, a, k).wait_recv())
        return dst[a].reshape(ROWS, LANES)

    def send_y(value, src, dst, send, recv, a):
        for i in range(NY):
            src[a, i] = value[i * 2 * NZ:(i + 1) * 2 * NZ].astype(BF16)
        each(NY, lambda k: y_copy(src, dst, send, recv, a, k).start())
        dst[a, y] = src[a, y]

    def take_y(src, dst, send, recv, a):
        each(NY, lambda k: y_come(src, dst, send, recv, a, k).wait_recv())
        return jnp.concatenate([dst[a, i].astype(F32) for i in range(NY)], axis=0).astype(BF16)

    def project_in(a, mat, p):
        lanes = pl.ds(pl.multiple_of(p * (LANES - TILE), 128), TILE)
        deep = pl.ds(pl.multiple_of((1 - p) * PAD, PAD), TILE)
        return dot(rows[a, :, lanes], mat[deep, :])

    def start_sum(a, mat):
        core_out[a] = project_in(a, mat, other).astype(BF16)
        c_copy(a).start()
        own[a] = project_in(a, mat, core)

    def next_sum(a):
        c_copy(a).wait_recv()
        total = own[a] + core_in[a].astype(F32)
        own[a] = total
        x_out[a] = total.astype(BF16).reshape(NX, PART, HW)
        each(NX, lambda k: x_copy(a, k).start())

    def end_sum(a):
        each(NX, lambda k: x_come(a, k).wait_recv())
        total = own[a, pl.ds(pl.multiple_of(x * PART, PART), PART), :]
        for off in range(1, NX):
            total = total + x_in[a, (x + NX - off) % NX].astype(F32)
        return total

    def start_gather(a, value):
        hid[a, core, x] = value.astype(BF16)
        each(NX, lambda k: g_copy(a, k).start())
        f_copy(a, 0).start()

    def next_gather(a):
        for k in (NX - 1, NX - 2, 1):
            g_come(a, k).wait_recv()
            f_copy(a, spread(k, NX)).start()

    def end_gather(a):
        for off in range(NX):
            f_come(a, off).wait_recv()

    def project_out(a, mat):
        left = dot(hid[a, 0].reshape(ROWS, HW), mat[pl.ds(PAD, TILE), :], 1, 1)
        right = dot(hid[a, 1].reshape(ROWS, HW), mat[pl.ds(0, TILE), :], 1, 1)
        cut = LANES - TILE
        return jnp.concatenate([left[:, :cut], left[:, cut:] + right[:, :TILE - cut], right[:, TILE - cut:]], axis=1)

    def weight_grad(a, h, out, hbm, sem):
        step = 256
        for n in range(HW // step):
            cols = pl.ds(n * step, step)
            left = dot(rows[a, :, pl.ds(0, TILE)], hid[h, 0, :, :, cols].reshape(ROWS, step), 0, 0)
            right = dot(rows[a, :, pl.ds(LANES - TILE, TILE)], hid[h, 1, :, :, cols].reshape(ROWS, step), 0, 0)
            grad_w[out, :, cols] = (left[:WIDTH] + right[PAD:]).astype(BF16)
        copy = pltpu.make_async_copy(grad_w.at[out], hbm, store_sem.at[out])
        copy.start()
        return copy

    def send_back(a, mat):
        send_y(project_out(a, mat), yb_out, yb_in, yb_send, yb_recv, a)

    def turn_back(a):
        got = take_y(yb_out, yb_in, yb_send, yb_recv, a)
        zb_out[a] = dot(perm_back[...], got).astype(BF16).reshape(NZ, 2 * NY, LANES)
        send_z(zb_out, zb_in, zb_send, zb_recv, a)

    def picked(a):
        got = take_z(zb_out, zb_in, zb_send, zb_recv, a)
        left = dot(got[:, :TILE], pick[0], 0, 0)
        right = dot(got[:, LANES - TILE:], pick[1], 0, 0)
        return left[:WIDTH] + right[PAD:]

    loads[0].wait()
    loads[1].wait()
    z_out[0] = dot(chosen, tok_src[...], 1, 1).astype(BF16).reshape(NZ, 2 * NY, LANES)
    pl.semaphore_wait(barrier, NZ + NY + NX + NCORE - 4)
    send_z(z_out, z_in, z_send, z_recv, 0)
    loads[2].wait()
    loads[3].wait()
    z_out[1] = (scale * dot(chosen, cot_src[...], 1, 1)).astype(BF16).reshape(NZ, 2 * NY, LANES)
    send_z(z_out, z_in, z_send, z_recv, 1)
    loads[4].wait()
    loads[5].wait()

    def turn(a):
        send_y(dot(perm_out[...], take_z(z_out, z_in, z_send, z_recv, a)), y_out, y_in, y_send, y_recv, a)

    turn(0)
    rows[0] = take_y(y_out, y_in, y_send, y_recv, 0)
    start_sum(0, gate_w)
    next_sum(0)
    turn(1)
    gate = end_sum(0)
    gate_keep[...] = gate
    start_gather(0, gate * jax.nn.sigmoid(gate))
    next_gather(0)
    end_gather(0)
    send_back(0, down_w)
    rows[1] = take_y(y_out, y_in, y_send, y_recv, 1)
    start_sum(1, down_w)
    next_sum(1)
    turn_back(0)
    wide = end_sum(1)
    gate = gate_keep[...]
    sig = jax.nn.sigmoid(gate)
    start_gather(1, wide * sig * (1.0 + gate * (1.0 - sig)))
    next_gather(1)
    end_gather(1)
    send_back(1, gate_w)
    stores = [weight_grad(0, 1, 0, gate_grad_hbm, store_sem)]
    turn_back(1)
    stores.append(weight_grad(1, 0, 1, down_grad_hbm, store_sem))
    both = picked(0)
    mixed_ref[...] = (both[:, :TOK] * weight_ref[0:1, :] + both[:, TOK:] * weight_ref[1:2, :]).astype(BF16)
    both = picked(1)
    grad_ref[...] = (both[:, :TOK] + both[:, TOK:]).astype(BF16)

    for a in range(2):
        each(NZ, lambda k: z_copy(z_out, z_in, z_send, z_recv, a, k).wait_send())
        each(NY, lambda k: y_copy(y_out, y_in, y_send, y_recv, a, k).wait_send())
        each(NX, lambda k: x_copy(a, k).wait_send())
        each(NX, lambda k: g_copy(a, k).wait_send())
        for off in range(NX):
            f_copy(a, off).wait_send()
        c_copy(a).wait_send()
        each(NY, lambda k: y_copy(yb_out, yb_in, yb_send, yb_recv, a, k).wait_send())
        each(NZ, lambda k: z_copy(zb_out, zb_in, zb_send, zb_recv, a, k).wait_send())
    for store in stores:
        store.wait()


def per_device(tokens, cotangent, slot_route, route_weight, w_gate, w_down):
    hbm, vmem = pl.BlockSpec(memory_space=pl.ANY), pl.BlockSpec(memory_space=pltpu.VMEM)
    dma = pltpu.SemaphoreType.DMA
    mixed, input_grad, gate_grad, down_grad = pl.pallas_call(
        layer,
        out_shape=(
            jax.ShapeDtypeStruct((WIDTH, TOK), BF16),
            jax.ShapeDtypeStruct((WIDTH, TOK), BF16),
            jax.ShapeDtypeStruct((WIDTH, HW), BF16),
            jax.ShapeDtypeStruct((WIDTH, HW), BF16),
        ),
        in_specs=[hbm, hbm, vmem, vmem, hbm, hbm],
        out_specs=(vmem, vmem, hbm, hbm),
        scratch_shapes=[
            pltpu.VMEM((LANES, 2 * TOK), BF16), pltpu.VMEM((LANES, 2 * TOK), BF16),
            pltpu.VMEM((WIDTH + 2 * PAD, HW), BF16), pltpu.VMEM((WIDTH + 2 * PAD, HW), BF16),
            pltpu.VMEM((2, ROWS, 2 * TOK), BF16),
            pltpu.VMEM((ROWS, ROWS), BF16), pltpu.VMEM((ROWS, ROWS), BF16),
            pltpu.VMEM((2, NZ, 2 * NY, LANES), BF16), pltpu.VMEM((2, NZ, 2 * NY, LANES), BF16),
            pltpu.VMEM((2, NY, 2 * NZ, LANES), BF16), pltpu.VMEM((2, NY, 2 * NZ, LANES), BF16),
            pltpu.VMEM((2, ROWS, LANES), BF16),
            pltpu.VMEM((2, ROWS, HW), BF16), pltpu.VMEM((2, ROWS, HW), BF16),
            pltpu.VMEM((2, ROWS, HW), F32),
            pltpu.VMEM((2, NX, PART, HW), BF16), pltpu.VMEM((2, NX, PART, HW), BF16),
            pltpu.VMEM((2, NCORE, NX, PART, HW), BF16),
            pltpu.VMEM((PART, HW), F32),
            pltpu.VMEM((2, NY, 2 * NZ, LANES), BF16), pltpu.VMEM((2, NY, 2 * NZ, LANES), BF16),
            pltpu.VMEM((2, NZ, 2 * NY, LANES), BF16), pltpu.VMEM((2, NZ, 2 * NY, LANES), BF16),
            pltpu.VMEM((2, WIDTH, HW), BF16),
            dma((6,)), dma((2,)),
            dma((2, NZ)), dma((2, NZ)), dma((2, NY)), dma((2, NY)), dma((2,)), dma((2,)),
            dma((2, NX)), dma((2, NX)), dma((2, NX)), dma((2, NX)), dma((2, NX)), dma((2, NX)),
            dma((2, NY)), dma((2, NY)), dma((2, NZ)), dma((2, NZ)),
        ],
        compiler_params=pltpu.CompilerParams(
            collective_id=0, has_side_effects=True, vmem_limit_bytes=48 * 1024 * 1024),
        name="moe_layer",
    )(tokens.T, cotangent.T, slot_route.T, route_weight.T, w_gate[0], w_down[0].T)
    return mixed.T, input_grad.T, gate_grad[None], down_grad.T[None]


def solution(mesh):
    return jax.shard_map(
        per_device,
        mesh=mesh,
        in_specs=(
            P("dp", "expert"),
            P("dp", "expert"),
            P("dp", None),
            P("dp", None),
            P("dp", "expert", None),
            P("dp", None, "expert"),
        ),
        out_specs=(
            P("dp", "expert"),
            P("dp", "expert"),
            P("dp", "expert", None),
            P("dp", None, "expert"),
        ),
        check_vma=False,
    )
```

```python
import jax
import jax.numpy as jnp
from jax import lax
from jax.experimental import pallas as pl
from jax.experimental.pallas import tpu as pltpu
from jax.sharding import PartitionSpec as P

NY, NZ, NX, NCORE = 8, 12, 4, 2
BF16, F32 = jnp.bfloat16, jnp.float32
MESH = pl.DeviceIdType.MESH
TOK = 128
WIDTH = 448
TILE = 512
LANES = 2 * WIDTH
ROWS = 2 * NY * NZ
HW = 1024
COLS = HW // NX
SETS = ((0, 3, 6, 9), (1, 5, 7, 11), (2, 4, 8, 10))
OFFSETS = SETS[0] + SETS[1] + SETS[2]
LEN = len(SETS[0])
CHUNK = ROWS // len(SETS)
UNITS = tuple((kind, chunk) for kind in range(2) for chunk in range(len(SETS)))
STEPS = (("turn", 0.0), ("sum", 4.0), ("sum_x", 6.2), ("act", 8.7), ("forward", 11.5), ("out", 12.3), ("back", 17.0))
BETWEEN = 3.7


def spread(k, n):
    return n // 2 + (k // 2) * (1 - 2 * (k % 2))


def dot(a, b, contract_a=1, contract_b=0):
    return lax.dot_general(a, b, (((contract_a,), (contract_b,)), ((), ())), preferred_element_type=F32)


def each(n, step):
    def one(k, carry):
        step(k)
        return carry

    lax.fori_loop(1, n, one, 0)


def layer(
    tok_hbm, cot_hbm, slot_ref, weight_ref, gate_hbm, down_hbm,
    mixed_ref, grad_ref, gate_grad_hbm, down_grad_hbm,
    tok_src, cot_src, gate_w, down_w, pick, perm_out, perm_back,
    z_out, z_in, y_out, y_in, rows,
    core_out, core_in, own, x_out, x_in, hid, gate_keep,
    yb_out, yb_in, zb_out, zb_in, weight_grads,
    load_sem, store_sem,
    z_send, z_recv, y_send, y_recv, c_send, c_recv, x_send, x_recv,
    g_send, g_recv, f_send, f_recv, yb_send, yb_recv, zb_send, zb_recv,
):
    dp, ex = lax.axis_index("dp"), lax.axis_index("expert")
    y, z = dp // NZ, dp % NZ
    x, core = ex // NCORE, ex % NCORE
    other = 1 - core
    mats = (gate_w, down_w)

    def at_z(off):
        return (y * NZ + (z + off) % NZ, ex)

    def at_y(k):
        return (((y + spread(k, NY)) % NY) * NZ + z, ex)

    def at_x(k):
        return (dp, ((x + spread(k, NX)) % NX) * NCORE + core)

    at_core = (dp, x * NCORE + other)

    barrier = pltpu.get_barrier_semaphore()

    def hello(to):
        pl.semaphore_signal(barrier, inc=1, device_id=to, device_id_type=MESH)

    each(NZ, lambda k: hello(at_z(k)))
    each(NY, lambda k: hello(at_y(k)))
    each(NX, lambda k: hello(at_x(k)))
    hello(at_core)

    loads = [
        pltpu.make_async_copy(tok_hbm, tok_src.at[pl.ds(0, WIDTH), pl.ds(0, TOK)], load_sem.at[0]),
        pltpu.make_async_copy(tok_hbm, tok_src.at[pl.ds(WIDTH, WIDTH), pl.ds(TOK, TOK)], load_sem.at[1]),
        pltpu.make_async_copy(cot_hbm, cot_src.at[pl.ds(0, WIDTH), pl.ds(0, TOK)], load_sem.at[2]),
        pltpu.make_async_copy(cot_hbm, cot_src.at[pl.ds(WIDTH, WIDTH), pl.ds(TOK, TOK)], load_sem.at[3]),
        pltpu.make_async_copy(gate_hbm, gate_w.at[pl.ds(0, WIDTH)], load_sem.at[4]),
        pltpu.make_async_copy(down_hbm, down_w.at[pl.ds(0, WIDTH)], load_sem.at[5]),
    ]
    for load in loads:
        load.start()

    for src in (tok_src, cot_src):
        src[pl.ds(0, WIDTH), pl.ds(TOK, TOK)] = jnp.zeros((WIDTH, TOK), BF16)
        src[pl.ds(WIDTH, WIDTH), pl.ds(0, TOK)] = jnp.zeros((WIDTH, TOK), BF16)

    inner = lax.broadcasted_iota(jnp.int32, (2 * NY, TOK), 0)
    to = jnp.concatenate([(inner >> 1) * NZ + (z + off) % NZ for off in OFFSETS], axis=0)
    odd = (lax.broadcasted_iota(jnp.int32, (ROWS, TOK), 0) & 1) == 1
    half = NY * NZ // 2
    slot = jnp.where(odd, 2 * jnp.where(to < half, to + half, to - half) + 1, 2 * to)
    is_0, is_1 = slot == slot_ref[0:1, :], slot == slot_ref[1:2, :]
    named = jnp.where(is_0 | is_1, 1.0, 0.0)
    earlier = lax.broadcasted_iota(jnp.int32, (TOK, TOK), 0) < lax.broadcasted_iota(jnp.int32, (TOK, TOK), 1)
    before = dot(named.astype(BF16), jnp.where(earlier, 1.0, 0.0).astype(BF16))
    first = jnp.where(before < 0.5, 1.0, 0.0)
    later = 1.0 - first
    chosen = jnp.concatenate([named * first, named * later], axis=1).astype(BF16)
    loads[0].wait()
    loads[1].wait()
    z_out[0] = dot(chosen, tok_src[...], 1, 1).astype(BF16).reshape(NZ, 2 * NY, LANES)
    pl.semaphore_wait(barrier, NZ + NY + NX + NCORE - 4)

    def z_copy(src, dst, send, recv, kind, q):
        return pltpu.make_async_remote_copy(
            src_ref=src.at[kind, q], dst_ref=dst.at[kind, q], send_sem=send.at[kind, q], recv_sem=recv.at[kind, q],
            device_id=at_z(OFFSETS[q]), device_id_type=MESH)

    def zb_copy(src, dst, send, recv, kind, q):
        return pltpu.make_async_remote_copy(
            src_ref=src.at[kind, q], dst_ref=dst.at[kind, q], send_sem=send.at[kind, q], recv_sem=recv.at[kind, q],
            device_id=at_z(NZ - OFFSETS[q]), device_id_type=MESH)

    def y_copy(src, dst, send, recv, u, k):
        off = spread(k, NY)
        return pltpu.make_async_remote_copy(
            src_ref=src.at[u[0], u[1], (y + off) % NY], dst_ref=dst.at[u[0], u[1], y], send_sem=send.at[u[0], u[1], off],
            recv_sem=recv.at[u[0], u[1], off], device_id=at_y(k), device_id_type=MESH)

    def y_come(src, dst, send, recv, u, k):
        off = spread(k, NY)
        return pltpu.make_async_remote_copy(
            src_ref=src.at[u[0], u[1], y], dst_ref=dst.at[u[0], u[1], (y + NY - off) % NY], send_sem=send.at[u[0], u[1], off],
            recv_sem=recv.at[u[0], u[1], off], device_id=at_y(k), device_id_type=MESH)

    def part(u):
        return pl.ds(u[1] * CHUNK, CHUNK)

    def hid_rows(u, position):
        return pl.ds(pl.multiple_of(u[1] * 2 * CHUNK + position * CHUNK, CHUNK), CHUNK)

    def x_copy(u, k):
        off = spread(k, NX)
        return pltpu.make_async_remote_copy(
            src_ref=x_out.at[u[0], (x + off) % NX, part(u)], dst_ref=x_in.at[u[0], x, part(u)], send_sem=x_send.at[u[0], u[1], off],
            recv_sem=x_recv.at[u[0], u[1], off], device_id=at_x(k), device_id_type=MESH)

    def x_come(u, k):
        off = spread(k, NX)
        return pltpu.make_async_remote_copy(
            src_ref=x_out.at[u[0], x, part(u)], dst_ref=x_in.at[u[0], (x + NX - off) % NX, part(u)], send_sem=x_send.at[u[0], u[1], off],
            recv_sem=x_recv.at[u[0], u[1], off], device_id=at_x(k), device_id_type=MESH)

    def g_copy(u, k):
        off = spread(k, NX)
        mine = hid.at[u[0], x, hid_rows(u, core)]
        return pltpu.make_async_remote_copy(
            src_ref=mine, dst_ref=mine, send_sem=g_send.at[u[0], u[1], off],
            recv_sem=g_recv.at[u[0], u[1], off], device_id=at_x(k), device_id_type=MESH)

    def g_come(u, k):
        off = spread(k, NX)
        return pltpu.make_async_remote_copy(
            src_ref=hid.at[u[0], x, hid_rows(u, core)], dst_ref=hid.at[u[0], (x + NX - off) % NX, hid_rows(u, core)],
            send_sem=g_send.at[u[0], u[1], off], recv_sem=g_recv.at[u[0], u[1], off], device_id=at_x(k), device_id_type=MESH)

    def f_copy(u, off):
        block = hid.at[u[0], (x + NX - off) % NX, hid_rows(u, core)]
        return pltpu.make_async_remote_copy(
            src_ref=block, dst_ref=block, send_sem=f_send.at[u[0], u[1], off],
            recv_sem=f_recv.at[u[0], u[1], off], device_id=at_core, device_id_type=MESH)

    def f_come(u, off):
        frm = (x + NX - off) % NX
        return pltpu.make_async_remote_copy(
            src_ref=hid.at[u[0], frm, hid_rows(u, core)], dst_ref=hid.at[u[0], frm, hid_rows(u, other)],
            send_sem=f_send.at[u[0], u[1], off], recv_sem=f_recv.at[u[0], u[1], off], device_id=at_core, device_id_type=MESH)

    def c_copy(u):
        return pltpu.make_async_remote_copy(
            src_ref=core_out.at[u[0], part(u)], dst_ref=core_in.at[u[0], part(u)], send_sem=c_send.at[u[0], u[1]],
            recv_sem=c_recv.at[u[0], u[1]], device_id=at_core, device_id_type=MESH)

    blocks = [[q for q in range(c * LEN, (c + 1) * LEN)] for c in range(len(SETS))]
    far = (NX - 1, NX - 2, 1)

    def send_z(u):
        for q in blocks[u[1]]:
            if OFFSETS[q]:
                z_copy(z_out, z_in, z_send, z_recv, u[0], q).start()
            else:
                z_in[u[0], q] = z_out[u[0], q]

    def send_y(value, src, dst, send, recv, u):
        src[u[0], u[1]] = value.reshape(NY, 2 * LEN, LANES).astype(BF16)
        each(NY, lambda k: y_copy(src, dst, send, recv, u, k).start())
        dst[u[0], u[1], y] = src[u[0], u[1], y]

    def take_y(src, dst, send, recv, u):
        each(NY, lambda k: y_come(src, dst, send, recv, u, k).wait_recv())
        return dst[u[0], u[1]].astype(F32).reshape(CHUNK, LANES)

    def turn(u):
        for q in blocks[u[1]]:
            if OFFSETS[q]:
                z_copy(z_out, z_in, z_send, z_recv, u[0], q).wait_recv()
        got = z_in[u[0], pl.ds(u[1] * LEN, LEN)].reshape(CHUNK, LANES)
        send_y(dot(perm_out[...], got), y_out, y_in, y_send, y_recv, u)

    def partial_sum(u):
        got = take_y(y_out, y_in, y_send, y_recv, u)
        right = pltpu.roll(got[:, LANES - TILE:], WIDTH, 1)
        both = jnp.concatenate([got[:, :TILE], right], axis=0).astype(BF16)
        rows[u[0], pl.ds(u[1] * 2 * CHUNK, 2 * CHUNK)] = both
        total = dot(both, mats[u[0]][...])
        low, high = total[:CHUNK], total[CHUNK:]
        core_out[u[0], part(u)] = jnp.where(core == 0, high, low).astype(BF16)
        c_copy(u).start()
        own[u[0], part(u)] = jnp.where(core == 0, low, high)

    def sum_x(u):
        c_copy(u).wait_recv()
        total = own[u[0], part(u)] + core_in[u[0], part(u)].astype(F32)
        own[u[0], part(u)] = total
        for i in range(NX):
            x_out[u[0], i, part(u)] = total[:, i * COLS:(i + 1) * COLS].astype(BF16)
        each(NX, lambda k: x_copy(u, k).start())

    def act(u):
        each(NX, lambda k: x_come(u, k).wait_recv())
        total = own[u[0], part(u), pl.ds(pl.multiple_of(x * COLS, COLS), COLS)]
        for off in range(1, NX):
            total = total + x_in[u[0], (x + NX - off) % NX, part(u)].astype(F32)
        if u[0] == 0:
            gate_keep[part(u)] = total
            value = total * jax.nn.sigmoid(total)
        else:
            gate = gate_keep[part(u)]
            sig = jax.nn.sigmoid(gate)
            value = total * sig * (1.0 + gate * (1.0 - sig))
        hid[u[0], x, hid_rows(u, core)] = value.astype(BF16)
        each(NX, lambda k: g_copy(u, k).start())
        f_copy(u, 0).start()

    def forward(u):
        for k in far:
            g_come(u, k).wait_recv()
            f_copy(u, spread(k, NX)).start()

    def out(u):
        for off in range(NX):
            f_come(u, off).wait_recv()
        both = pl.ds(u[1] * 2 * CHUNK, 2 * CHUNK)
        value = jnp.concatenate([hid[u[0], i, both] for i in range(NX)], axis=1)
        value = dot(value, mats[1 - u[0]][...], 1, 1)
        left, right = value[:CHUNK], pltpu.roll(value[CHUNK:], TILE - WIDTH, 1)
        cut = LANES - TILE
        value = jnp.concatenate([left[:, :cut], left[:, cut:] + right[:, :TILE - cut], right[:, TILE - cut:]], axis=1)
        send_y(value, yb_out, yb_in, yb_send, yb_recv, u)

    def back(u):
        got = take_y(yb_out, yb_in, yb_send, yb_recv, u).astype(BF16)
        zb_out[u[0], pl.ds(u[1] * LEN, LEN)] = dot(perm_back[...], got).astype(BF16).reshape(LEN, 2 * NY, LANES)
        for q in blocks[u[1]]:
            if OFFSETS[q]:
                zb_copy(zb_out, zb_in, zb_send, zb_recv, u[0], q).start()
            else:
                zb_in[u[0], q] = zb_out[u[0], q]

    def picked(kind, c, n):
        for q in range(c * LEN, (c + n) * LEN):
            if OFFSETS[q]:
                zb_copy(zb_out, zb_in, zb_send, zb_recv, kind, q).wait_recv()
        got = zb_in[kind, pl.ds(c * LEN, n * LEN)].reshape(n * CHUNK, LANES)
        here = pl.ds(c * CHUNK, n * CHUNK)
        left = dot(got[:, :TILE], pick[0, here], 0, 0)
        right = dot(got[:, LANES - TILE:], pick[1, here], 0, 0)
        return left[:WIDTH] + right[TILE - WIDTH:]

    stores = [
        pltpu.make_async_copy(weight_grads.at[kind], result, store_sem.at[kind])
        for kind, result in enumerate((gate_grad_hbm, down_grad_hbm))]

    def weight_grad(kind):
        for i in range(NX):
            grad = dot(rows[kind], hid[1 - kind, i], 0, 0)
            weight_grads[kind, :, pl.ds(i * COLS, COLS)] = grad[:WIDTH].astype(BF16)
        stores[kind].start()

    send_z(UNITS[0])
    send_z(UNITS[1])
    one_0, one_1 = jnp.where(is_0, 1.0, 0.0), jnp.where(is_1, 1.0, 0.0)
    weight_of = one_0 * weight_ref[0:1, :] + one_1 * weight_ref[1:2, :]
    scale_first = jnp.sum(weight_of * first, axis=1, keepdims=True)
    scale_later = jnp.sum(weight_of * later, axis=1, keepdims=True)
    lane = lax.broadcasted_iota(jnp.int32, (ROWS, LANES), 1)
    scale = jnp.where(lane < WIDTH, scale_first, scale_later)
    loads[2].wait()
    loads[3].wait()
    z_out[1] = (scale * dot(chosen, cot_src[...], 1, 1)).astype(BF16).reshape(NZ, 2 * NY, LANES)
    pick[0] = jnp.concatenate([one_0 * first, one_1 * first], axis=1).astype(BF16)
    pick[1] = jnp.concatenate([one_0 * later, one_1 * later], axis=1).astype(BF16)
    down_axis = lax.broadcasted_iota(jnp.int32, (CHUNK, CHUNK), 0)
    along_axis = lax.broadcasted_iota(jnp.int32, (CHUNK, CHUNK), 1)

    def place(c):
        return ((c >> 1) & (NY - 1)) * (2 * LEN) + (c >> 4) * 2 + (c & 1)

    perm_out[...] = jnp.where(down_axis == place(along_axis), 1.0, 0.0).astype(BF16)
    perm_back[...] = jnp.where(place(down_axis) == along_axis, 1.0, 0.0).astype(BF16)
    for mat in mats:
        mat[pl.ds(WIDTH, TILE - WIDTH), :] = jnp.zeros((TILE - WIDTH, HW), BF16)
    loads[4].wait()
    loads[5].wait()

    names = dict(turn=turn, sum=partial_sum, sum_x=sum_x, act=act, forward=forward, out=out, back=back)
    plan = sorted(
        ((n * BETWEEN + at, n, name) for n in range(len(UNITS)) for name, at in STEPS), key=lambda e: e[:2])
    for _, n, name in plan:
        if name == "turn" and n + 2 < len(UNITS):
            send_z(UNITS[n + 2])
        names[name](UNITS[n])
        if name == "out" and n == len(UNITS) - 1:
            weight_grad(1)
    weight_grad(0)
    both = picked(0, 0, len(SETS))
    mixed_ref[...] = (both[:, :TOK] * weight_ref[0:1, :] + both[:, TOK:] * weight_ref[1:2, :]).astype(BF16)
    both = picked(1, 0, len(SETS) - 1)
    both = both + picked(1, len(SETS) - 1, 1)
    grad_ref[...] = (both[:, :TOK] + both[:, TOK:]).astype(BF16)

    for u in UNITS:
        for q in blocks[u[1]]:
            if OFFSETS[q]:
                z_copy(z_out, z_in, z_send, z_recv, u[0], q).wait_send()
                zb_copy(zb_out, zb_in, zb_send, zb_recv, u[0], q).wait_send()
        each(NY, lambda k: y_copy(y_out, y_in, y_send, y_recv, u, k).wait_send())
        each(NY, lambda k: y_copy(yb_out, yb_in, yb_send, yb_recv, u, k).wait_send())
        each(NX, lambda k: x_copy(u, k).wait_send())
        each(NX, lambda k: g_copy(u, k).wait_send())
        for off in range(NX):
            f_copy(u, off).wait_send()
        c_copy(u).wait_send()
    for store in stores:
        store.wait()


def write(*refs):
    n = len(refs) // 2
    copies = [pltpu.make_async_copy(refs[i], refs[n + i], refs[2 * n].at[i]) for i in range(n)]
    for copy in copies:
        copy.start()
    for copy in copies:
        copy.wait()


def per_device(tokens, cotangent, slot_route, route_weight, w_gate, w_down):
    hbm, vmem = pl.BlockSpec(memory_space=pltpu.HBM), pl.BlockSpec(memory_space=pltpu.VMEM)
    dma = pltpu.SemaphoreType.DMA
    chunks = len(SETS)
    shapes = (
        jax.ShapeDtypeStruct((WIDTH, TOK), BF16),
        jax.ShapeDtypeStruct((WIDTH, TOK), BF16),
        jax.ShapeDtypeStruct((WIDTH, HW), BF16),
        jax.ShapeDtypeStruct((WIDTH, HW), BF16),
    )
    results = pl.pallas_call(
        layer,
        out_shape=shapes,
        in_specs=[hbm, hbm, vmem, vmem, hbm, hbm],
        out_specs=(vmem, vmem, hbm, hbm),
        scratch_shapes=[
            pltpu.VMEM((LANES, 2 * TOK), BF16), pltpu.VMEM((LANES, 2 * TOK), BF16),
            pltpu.VMEM((TILE, HW), BF16), pltpu.VMEM((TILE, HW), BF16),
            pltpu.VMEM((2, ROWS, 2 * TOK), BF16),
            pltpu.VMEM((CHUNK, CHUNK), BF16), pltpu.VMEM((CHUNK, CHUNK), BF16),
            pltpu.VMEM((2, NZ, 2 * NY, LANES), BF16), pltpu.VMEM((2, NZ, 2 * NY, LANES), BF16),
            pltpu.VMEM((2, chunks, NY, 2 * LEN, LANES), BF16), pltpu.VMEM((2, chunks, NY, 2 * LEN, LANES), BF16),
            pltpu.VMEM((2, 2 * ROWS, TILE), BF16),
            pltpu.VMEM((2, ROWS, HW), BF16), pltpu.VMEM((2, ROWS, HW), BF16),
            pltpu.VMEM((2, ROWS, HW), F32),
            pltpu.VMEM((2, NX, ROWS, COLS), BF16), pltpu.VMEM((2, NX, ROWS, COLS), BF16),
            pltpu.VMEM((2, NX, 2 * ROWS, COLS), BF16),
            pltpu.VMEM((ROWS, COLS), F32),
            pltpu.VMEM((2, chunks, NY, 2 * LEN, LANES), BF16), pltpu.VMEM((2, chunks, NY, 2 * LEN, LANES), BF16),
            pltpu.VMEM((2, NZ, 2 * NY, LANES), BF16), pltpu.VMEM((2, NZ, 2 * NY, LANES), BF16),
            pltpu.VMEM((2, WIDTH, HW), BF16),
            dma((6,)), dma((2,)),
            dma((2, NZ)), dma((2, NZ)), dma((2, chunks, NY)), dma((2, chunks, NY)), dma((2, chunks)), dma((2, chunks)),
            dma((2, chunks, NX)), dma((2, chunks, NX)), dma((2, chunks, NX)), dma((2, chunks, NX)),
            dma((2, chunks, NX)), dma((2, chunks, NX)),
            dma((2, chunks, NY)), dma((2, chunks, NY)), dma((2, NZ)), dma((2, NZ)),
        ],
        compiler_params=pltpu.CompilerParams(
            collective_id=0, has_side_effects=True, vmem_limit_bytes=58 * 1024 * 1024),
        name="moe_layer",
    )(tokens.T, cotangent.T, slot_route.T, route_weight.T, w_gate[0], w_down[0].T)
    mixed, input_grad, gate_grad, down_grad = pl.pallas_call(
        write,
        out_shape=shapes,
        in_specs=[vmem] * 4,
        out_specs=(hbm,) * 4,
        scratch_shapes=[dma((4,))],
        name="write_results",
    )(*results)
    return mixed.T, input_grad.T, gate_grad[None], down_grad.T[None]


def solution(mesh):
    return jax.shard_map(
        per_device,
        mesh=mesh,
        in_specs=(
            P("dp", "expert"),
            P("dp", "expert"),
            P("dp", None),
            P("dp", None),
            P("dp", "expert", None),
            P("dp", None, "expert"),
        ),
        out_specs=(
            P("dp", "expert"),
            P("dp", "expert"),
            P("dp", "expert", None),
            P("dp", None, "expert"),
        ),
        check_vma=False,
    )
```

```python
import jax
import jax.numpy as jnp
from jax import lax
from jax.experimental import pallas as pl
from jax.experimental.pallas import tpu as pltpu
from jax.sharding import PartitionSpec as P

NY, NZ, NX, NCORE = 8, 12, 4, 2
BF16, F32 = jnp.bfloat16, jnp.float32
MESH = pl.DeviceIdType.MESH
TOK = 128
WIDTH = 448
TILE = 512
LANES = 2 * WIDTH
ROWS = 2 * NY * NZ
HW = 1024
COLS = HW // NX
SETS = ((0, 3, 6, 9), (1, 5, 7, 11), (2, 4, 8, 10))
OFFSETS = SETS[0] + SETS[1] + SETS[2]
LEN = len(SETS[0])
CHUNK = ROWS // len(SETS)
UNITS = tuple((kind, chunk) for kind in range(2) for chunk in range(len(SETS)))
STEPS = (("turn", 0.0), ("sum", 8.5), ("sum_x", 11.0), ("act", 15.5), ("forward", 20.0), ("out", 22.0), ("back", 30.0))
BETWEEN = 3.7


def spread(k, n):
    return n // 2 + (k // 2) * (1 - 2 * (k % 2))


def dot(a, b, contract_a=1, contract_b=0):
    return lax.dot_general(a, b, (((contract_a,), (contract_b,)), ((), ())), preferred_element_type=F32)


def each(n, step):
    for k in range(1, n):
        step(k)


def layer(
    tok_hbm, cot_hbm, slot_ref, weight_ref, gate_hbm, down_hbm,
    mixed_ref, grad_ref, gate_grad_hbm, down_grad_hbm,
    tok_src, cot_src, gate_w, down_w, pick, perm_out, perm_back,
    z_out, z_in, y_out, y_in, rows,
    core_out, core_in, own, x_out, x_in, hid, gate_keep,
    yb_out, yb_in, zb_out, zb_in, weight_grads,
    load_sem, store_sem,
    z_send, z_recv, y_send, y_recv, c_send, c_recv, x_send, x_recv,
    g_send, g_recv, f_send, f_recv, yb_send, yb_recv, zb_send, zb_recv,
):
    dp, ex = lax.axis_index("dp"), lax.axis_index("expert")
    y, z = dp // NZ, dp % NZ
    x, core = ex // NCORE, ex % NCORE
    other = 1 - core
    mats = (gate_w, down_w)

    def at_z(off):
        return (y * NZ + (z + off) % NZ, ex)

    def at_y(k):
        return (((y + spread(k, NY)) % NY) * NZ + z, ex)

    def at_x(k):
        return (dp, ((x + spread(k, NX)) % NX) * NCORE + core)

    at_core = (dp, x * NCORE + other)

    barrier = pltpu.get_barrier_semaphore()

    def hello(to):
        pl.semaphore_signal(barrier, inc=1, device_id=to, device_id_type=MESH)

    each(NZ, lambda k: hello(at_z(k)))
    each(NY, lambda k: hello(at_y(k)))
    each(NX, lambda k: hello(at_x(k)))
    hello(at_core)

    loads = [
        pltpu.make_async_copy(tok_hbm, tok_src.at[pl.ds(0, WIDTH), pl.ds(0, TOK)], load_sem.at[0]),
        pltpu.make_async_copy(tok_hbm, tok_src.at[pl.ds(WIDTH, WIDTH), pl.ds(TOK, TOK)], load_sem.at[1]),
        pltpu.make_async_copy(cot_hbm, cot_src.at[pl.ds(0, WIDTH), pl.ds(0, TOK)], load_sem.at[2]),
        pltpu.make_async_copy(cot_hbm, cot_src.at[pl.ds(WIDTH, WIDTH), pl.ds(TOK, TOK)], load_sem.at[3]),
        pltpu.make_async_copy(gate_hbm, gate_w.at[pl.ds(0, WIDTH)], load_sem.at[4]),
        pltpu.make_async_copy(down_hbm, down_w.at[pl.ds(0, WIDTH)], load_sem.at[5]),
    ]
    for load in loads:
        load.start()

    for src in (tok_src, cot_src):
        src[pl.ds(0, WIDTH), pl.ds(TOK, TOK)] = jnp.zeros((WIDTH, TOK), BF16)
        src[pl.ds(WIDTH, WIDTH), pl.ds(0, TOK)] = jnp.zeros((WIDTH, TOK), BF16)

    inner = lax.broadcasted_iota(jnp.int32, (2 * NY, TOK), 0)
    to = jnp.concatenate([(inner >> 1) * NZ + (z + off) % NZ for off in OFFSETS], axis=0)
    odd = (lax.broadcasted_iota(jnp.int32, (ROWS, TOK), 0) & 1) == 1
    half = NY * NZ // 2
    slot = jnp.where(odd, 2 * jnp.where(to < half, to + half, to - half) + 1, 2 * to)
    is_0, is_1 = slot == slot_ref[0:1, :], slot == slot_ref[1:2, :]
    named = jnp.where(is_0 | is_1, 1.0, 0.0)
    earlier = lax.broadcasted_iota(jnp.int32, (TOK, TOK), 0) < lax.broadcasted_iota(jnp.int32, (TOK, TOK), 1)
    before = dot(named.astype(BF16), jnp.where(earlier, 1.0, 0.0).astype(BF16))
    first = jnp.where(before < 0.5, 1.0, 0.0)
    later = 1.0 - first
    chosen = jnp.concatenate([named * first, named * later], axis=1).astype(BF16)
    loads[0].wait()
    loads[1].wait()
    z_out[0] = dot(chosen, tok_src[...], 1, 1).astype(BF16).reshape(NZ, 2 * NY, LANES)
    pl.semaphore_wait(barrier, NZ + NY + NX + NCORE - 4)

    def z_copy(src, dst, send, recv, kind, q):
        return pltpu.make_async_remote_copy(
            src_ref=src.at[kind, q], dst_ref=dst.at[kind, q], send_sem=send.at[kind, q], recv_sem=recv.at[kind, q],
            device_id=at_z(OFFSETS[q]), device_id_type=MESH)

    def zb_copy(src, dst, send, recv, kind, q):
        return pltpu.make_async_remote_copy(
            src_ref=src.at[kind, q], dst_ref=dst.at[kind, q], send_sem=send.at[kind, q], recv_sem=recv.at[kind, q],
            device_id=at_z(NZ - OFFSETS[q]), device_id_type=MESH)

    def y_copy(src, dst, send, recv, u, k):
        off = spread(k, NY)
        return pltpu.make_async_remote_copy(
            src_ref=src.at[u[0], u[1], (y + off) % NY], dst_ref=dst.at[u[0], u[1], y], send_sem=send.at[u[0], u[1], off],
            recv_sem=recv.at[u[0], u[1], off], device_id=at_y(k), device_id_type=MESH)

    def y_come(src, dst, send, recv, u, k):
        off = spread(k, NY)
        return pltpu.make_async_remote_copy(
            src_ref=src.at[u[0], u[1], y], dst_ref=dst.at[u[0], u[1], (y + NY - off) % NY], send_sem=send.at[u[0], u[1], off],
            recv_sem=recv.at[u[0], u[1], off], device_id=at_y(k), device_id_type=MESH)

    def part(u):
        return pl.ds(u[1] * CHUNK, CHUNK)

    def hid_rows(u, position):
        return pl.ds(pl.multiple_of(u[1] * 2 * CHUNK + position * CHUNK, CHUNK), CHUNK)

    def x_copy(u, k):
        off = spread(k, NX)
        return pltpu.make_async_remote_copy(
            src_ref=x_out.at[u[0], (x + off) % NX, part(u)], dst_ref=x_in.at[u[0], x, part(u)], send_sem=x_send.at[u[0], u[1], off],
            recv_sem=x_recv.at[u[0], u[1], off], device_id=at_x(k), device_id_type=MESH)

    def x_come(u, k):
        off = spread(k, NX)
        return pltpu.make_async_remote_copy(
            src_ref=x_out.at[u[0], x, part(u)], dst_ref=x_in.at[u[0], (x + NX - off) % NX, part(u)], send_sem=x_send.at[u[0], u[1], off],
            recv_sem=x_recv.at[u[0], u[1], off], device_id=at_x(k), device_id_type=MESH)

    def g_copy(u, k):
        off = spread(k, NX)
        mine = hid.at[u[0], x, hid_rows(u, core)]
        return pltpu.make_async_remote_copy(
            src_ref=mine, dst_ref=mine, send_sem=g_send.at[u[0], u[1], off],
            recv_sem=g_recv.at[u[0], u[1], off], device_id=at_x(k), device_id_type=MESH)

    def g_come(u, k):
        off = spread(k, NX)
        return pltpu.make_async_remote_copy(
            src_ref=hid.at[u[0], x, hid_rows(u, core)], dst_ref=hid.at[u[0], (x + NX - off) % NX, hid_rows(u, core)],
            send_sem=g_send.at[u[0], u[1], off], recv_sem=g_recv.at[u[0], u[1], off], device_id=at_x(k), device_id_type=MESH)

    def f_copy(u):
        block = hid.at[u[0], :, hid_rows(u, core)]
        return pltpu.make_async_remote_copy(
            src_ref=block, dst_ref=block, send_sem=f_send.at[u[0], u[1]],
            recv_sem=f_recv.at[u[0], u[1]], device_id=at_core, device_id_type=MESH)

    def f_come(u):
        return pltpu.make_async_remote_copy(
            src_ref=hid.at[u[0], :, hid_rows(u, core)], dst_ref=hid.at[u[0], :, hid_rows(u, other)],
            send_sem=f_send.at[u[0], u[1]], recv_sem=f_recv.at[u[0], u[1]], device_id=at_core, device_id_type=MESH)

    def c_copy(u):
        return pltpu.make_async_remote_copy(
            src_ref=core_out.at[u[0], part(u)], dst_ref=core_in.at[u[0], part(u)], send_sem=c_send.at[u[0], u[1]],
            recv_sem=c_recv.at[u[0], u[1]], device_id=at_core, device_id_type=MESH)

    blocks = [[q for q in range(c * LEN, (c + 1) * LEN)] for c in range(len(SETS))]
    far = (NX - 1, NX - 2, 1)

    def send_z(u):
        for q in blocks[u[1]]:
            if OFFSETS[q]:
                z_copy(z_out, z_in, z_send, z_recv, u[0], q).start()
            else:
                z_in[u[0], q] = z_out[u[0], q]

    def send_y(value, src, dst, send, recv, u):
        src[u[0], u[1]] = value.reshape(NY, 2 * LEN, LANES).astype(BF16)
        each(NY, lambda k: y_copy(src, dst, send, recv, u, k).start())
        dst[u[0], u[1], y] = src[u[0], u[1], y]

    def take_y(src, dst, send, recv, u):
        each(NY, lambda k: y_come(src, dst, send, recv, u, k).wait_recv())
        return dst[u[0], u[1]].astype(F32).reshape(CHUNK, LANES)

    def turn(u):
        for q in blocks[u[1]]:
            if OFFSETS[q]:
                z_copy(z_out, z_in, z_send, z_recv, u[0], q).wait_recv()
        got = z_in[u[0], pl.ds(u[1] * LEN, LEN)].reshape(CHUNK, LANES)
        send_y(dot(perm_out[...], got), y_out, y_in, y_send, y_recv, u)

    def partial_sum(u):
        got = take_y(y_out, y_in, y_send, y_recv, u)
        right = pltpu.roll(got[:, LANES - TILE:], WIDTH, 1)
        both = jnp.concatenate([got[:, :TILE], right], axis=0).astype(BF16)
        rows[u[0], pl.ds(u[1] * 2 * CHUNK, 2 * CHUNK)] = both
        total = dot(both, mats[u[0]][...])
        low, high = total[:CHUNK], total[CHUNK:]
        core_out[u[0], part(u)] = jnp.where(core == 0, high, low).astype(BF16)
        c_copy(u).start()
        own[u[0], part(u)] = jnp.where(core == 0, low, high)

    def sum_x(u):
        c_copy(u).wait_recv()
        total = own[u[0], part(u)] + core_in[u[0], part(u)].astype(F32)
        own[u[0], part(u)] = total
        for i in range(NX):
            x_out[u[0], i, part(u)] = total[:, i * COLS:(i + 1) * COLS].astype(BF16)
        each(NX, lambda k: x_copy(u, k).start())

    def act(u):
        each(NX, lambda k: x_come(u, k).wait_recv())
        total = own[u[0], part(u), pl.ds(pl.multiple_of(x * COLS, COLS), COLS)]
        for off in range(1, NX):
            total = total + x_in[u[0], (x + NX - off) % NX, part(u)].astype(F32)
        if u[0] == 0:
            gate_keep[part(u)] = total
            value = total * jax.nn.sigmoid(total)
        else:
            gate = gate_keep[part(u)]
            sig = jax.nn.sigmoid(gate)
            value = total * sig * (1.0 + gate * (1.0 - sig))
        hid[u[0], x, hid_rows(u, core)] = value.astype(BF16)
        each(NX, lambda k: g_copy(u, k).start())

    def forward(u):
        for k in far:
            g_come(u, k).wait_recv()
        f_copy(u).start()

    def out(u):
        f_come(u).wait_recv()
        both = pl.ds(u[1] * 2 * CHUNK, 2 * CHUNK)
        value = jnp.concatenate([hid[u[0], i, both] for i in range(NX)], axis=1)
        value = dot(value, mats[1 - u[0]][...], 1, 1)
        left, right = value[:CHUNK], pltpu.roll(value[CHUNK:], TILE - WIDTH, 1)
        cut = LANES - TILE
        value = jnp.concatenate([left[:, :cut], left[:, cut:] + right[:, :TILE - cut], right[:, TILE - cut:]], axis=1)
        send_y(value, yb_out, yb_in, yb_send, yb_recv, u)

    def back(u):
        got = take_y(yb_out, yb_in, yb_send, yb_recv, u).astype(BF16)
        zb_out[u[0], pl.ds(u[1] * LEN, LEN)] = dot(perm_back[...], got).astype(BF16).reshape(LEN, 2 * NY, LANES)
        for q in blocks[u[1]]:
            if OFFSETS[q]:
                zb_copy(zb_out, zb_in, zb_send, zb_recv, u[0], q).start()
            else:
                zb_in[u[0], q] = zb_out[u[0], q]

    def picked(kind, c, n):
        for q in range(c * LEN, (c + n) * LEN):
            if OFFSETS[q]:
                zb_copy(zb_out, zb_in, zb_send, zb_recv, kind, q).wait_recv()
        got = zb_in[kind, pl.ds(c * LEN, n * LEN)].reshape(n * CHUNK, LANES)
        here = pl.ds(c * CHUNK, n * CHUNK)
        left = dot(got[:, :TILE], pick[0, here], 0, 0)
        right = dot(got[:, LANES - TILE:], pick[1, here], 0, 0)
        return left[:WIDTH] + right[TILE - WIDTH:]

    stores = [
        pltpu.make_async_copy(weight_grads.at[kind], result, store_sem.at[kind])
        for kind, result in enumerate((gate_grad_hbm, down_grad_hbm))]

    def weight_grad(kind):
        for i in range(NX):
            grad = dot(rows[kind], hid[1 - kind, i], 0, 0)
            weight_grads[kind, :, pl.ds(i * COLS, COLS)] = grad[:WIDTH].astype(BF16)
        stores[kind].start()

    send_z(UNITS[0])
    send_z(UNITS[1])
    one_0, one_1 = jnp.where(is_0, 1.0, 0.0), jnp.where(is_1, 1.0, 0.0)
    weight_of = one_0 * weight_ref[0:1, :] + one_1 * weight_ref[1:2, :]
    scale_first = jnp.sum(weight_of * first, axis=1, keepdims=True)
    scale_later = jnp.sum(weight_of * later, axis=1, keepdims=True)
    lane = lax.broadcasted_iota(jnp.int32, (ROWS, LANES), 1)
    scale = jnp.where(lane < WIDTH, scale_first, scale_later)
    loads[2].wait()
    loads[3].wait()
    z_out[1] = (scale * dot(chosen, cot_src[...], 1, 1)).astype(BF16).reshape(NZ, 2 * NY, LANES)
    pick[0] = jnp.concatenate([one_0 * first, one_1 * first], axis=1).astype(BF16)
    pick[1] = jnp.concatenate([one_0 * later, one_1 * later], axis=1).astype(BF16)
    down_axis = lax.broadcasted_iota(jnp.int32, (CHUNK, CHUNK), 0)
    along_axis = lax.broadcasted_iota(jnp.int32, (CHUNK, CHUNK), 1)

    def place(c):
        return ((c >> 1) & (NY - 1)) * (2 * LEN) + (c >> 4) * 2 + (c & 1)

    perm_out[...] = jnp.where(down_axis == place(along_axis), 1.0, 0.0).astype(BF16)
    perm_back[...] = jnp.where(place(down_axis) == along_axis, 1.0, 0.0).astype(BF16)
    for mat in mats:
        mat[pl.ds(WIDTH, TILE - WIDTH), :] = jnp.zeros((TILE - WIDTH, HW), BF16)
    loads[4].wait()
    loads[5].wait()

    names = dict(turn=turn, sum=partial_sum, sum_x=sum_x, act=act, forward=forward, out=out, back=back)
    plan = sorted(
        ((n * BETWEEN + at, n, name) for n in range(len(UNITS)) for name, at in STEPS), key=lambda e: e[:2])
    for _, n, name in plan:
        names[name](UNITS[n])
        if name == "turn" and n + 2 < len(UNITS):
            send_z(UNITS[n + 2])
        if name == "out" and n == len(UNITS) - 1:
            weight_grad(1)
    weight_grad(0)
    both = picked(0, 0, len(SETS))
    mixed_ref[...] = (both[:, :TOK] * weight_ref[0:1, :] + both[:, TOK:] * weight_ref[1:2, :]).astype(BF16)
    both = picked(1, 0, len(SETS) - 1)
    both = both + picked(1, len(SETS) - 1, 1)
    grad_ref[...] = (both[:, :TOK] + both[:, TOK:]).astype(BF16)

    for u in UNITS:
        for q in blocks[u[1]]:
            if OFFSETS[q]:
                z_copy(z_out, z_in, z_send, z_recv, u[0], q).wait_send()
                zb_copy(zb_out, zb_in, zb_send, zb_recv, u[0], q).wait_send()
        each(NY, lambda k: y_copy(y_out, y_in, y_send, y_recv, u, k).wait_send())
        each(NY, lambda k: y_copy(yb_out, yb_in, yb_send, yb_recv, u, k).wait_send())
        each(NX, lambda k: x_copy(u, k).wait_send())
        each(NX, lambda k: g_copy(u, k).wait_send())
        f_copy(u).wait_send()
        c_copy(u).wait_send()
    for store in stores:
        store.wait()


def write(*refs):
    n = len(refs) // 2
    copies = [pltpu.make_async_copy(refs[i], refs[n + i], refs[2 * n].at[i]) for i in range(n)]
    for copy in copies:
        copy.start()
    for copy in copies:
        copy.wait()


def per_device(tokens, cotangent, slot_route, route_weight, w_gate, w_down):
    hbm, vmem = pl.BlockSpec(memory_space=pltpu.HBM), pl.BlockSpec(memory_space=pltpu.VMEM)
    dma = pltpu.SemaphoreType.DMA
    chunks = len(SETS)
    shapes = (
        jax.ShapeDtypeStruct((WIDTH, TOK), BF16),
        jax.ShapeDtypeStruct((WIDTH, TOK), BF16),
        jax.ShapeDtypeStruct((WIDTH, HW), BF16),
        jax.ShapeDtypeStruct((WIDTH, HW), BF16),
    )
    results = pl.pallas_call(
        layer,
        out_shape=shapes,
        in_specs=[hbm, hbm, vmem, vmem, hbm, hbm],
        out_specs=(vmem, vmem, hbm, hbm),
        scratch_shapes=[
            pltpu.VMEM((LANES, 2 * TOK), BF16), pltpu.VMEM((LANES, 2 * TOK), BF16),
            pltpu.VMEM((TILE, HW), BF16), pltpu.VMEM((TILE, HW), BF16),
            pltpu.VMEM((2, ROWS, 2 * TOK), BF16),
            pltpu.VMEM((CHUNK, CHUNK), BF16), pltpu.VMEM((CHUNK, CHUNK), BF16),
            pltpu.VMEM((2, NZ, 2 * NY, LANES), BF16), pltpu.VMEM((2, NZ, 2 * NY, LANES), BF16),
            pltpu.VMEM((2, chunks, NY, 2 * LEN, LANES), BF16), pltpu.VMEM((2, chunks, NY, 2 * LEN, LANES), BF16),
            pltpu.VMEM((2, 2 * ROWS, TILE), BF16),
            pltpu.VMEM((2, ROWS, HW), BF16), pltpu.VMEM((2, ROWS, HW), BF16),
            pltpu.VMEM((2, ROWS, HW), F32),
            pltpu.VMEM((2, NX, ROWS, COLS), BF16), pltpu.VMEM((2, NX, ROWS, COLS), BF16),
            pltpu.VMEM((2, NX, 2 * ROWS, COLS), BF16),
            pltpu.VMEM((ROWS, COLS), F32),
            pltpu.VMEM((2, chunks, NY, 2 * LEN, LANES), BF16), pltpu.VMEM((2, chunks, NY, 2 * LEN, LANES), BF16),
            pltpu.VMEM((2, NZ, 2 * NY, LANES), BF16), pltpu.VMEM((2, NZ, 2 * NY, LANES), BF16),
            pltpu.VMEM((2, WIDTH, HW), BF16),
            dma((6,)), dma((2,)),
            dma((2, NZ)), dma((2, NZ)), dma((2, chunks, NY)), dma((2, chunks, NY)), dma((2, chunks)), dma((2, chunks)),
            dma((2, chunks, NX)), dma((2, chunks, NX)), dma((2, chunks, NX)), dma((2, chunks, NX)),
            dma((2, chunks)), dma((2, chunks)),
            dma((2, chunks, NY)), dma((2, chunks, NY)), dma((2, NZ)), dma((2, NZ)),
        ],
        compiler_params=pltpu.CompilerParams(
            collective_id=0, has_side_effects=True, vmem_limit_bytes=58 * 1024 * 1024),
        name="moe_layer",
    )(tokens.T, cotangent.T, slot_route.T, route_weight.T, w_gate[0], w_down[0].T)
    mixed, input_grad, gate_grad, down_grad = pl.pallas_call(
        write,
        out_shape=shapes,
        in_specs=[vmem] * 4,
        out_specs=(hbm,) * 4,
        scratch_shapes=[dma((4,))],
        name="write_results",
    )(*results)
    return mixed.T, input_grad.T, gate_grad[None], down_grad.T[None]


def solution(mesh):
    return jax.shard_map(
        per_device,
        mesh=mesh,
        in_specs=(
            P("dp", "expert"),
            P("dp", "expert"),
            P("dp", None),
            P("dp", None),
            P("dp", "expert", None),
            P("dp", None, "expert"),
        ),
        out_specs=(
            P("dp", "expert"),
            P("dp", "expert"),
            P("dp", "expert", None),
            P("dp", None, "expert"),
        ),
        check_vma=False,
    )
```

```python
import jax
import jax.numpy as jnp
from jax import lax
from jax.experimental import pallas as pl
from jax.experimental.pallas import tpu as pltpu
from jax.sharding import PartitionSpec as P

NY, NZ, NX, NCORE = 8, 12, 4, 2
BF16, F32 = jnp.bfloat16, jnp.float32
MESH = pl.DeviceIdType.MESH
TOK = 128
WIDTH = 448
TILE = 512
LANES = 2 * WIDTH
ROWS = 2 * NY * NZ
HW = 1024
COLS = HW // NX
SETS = ((1, 5, 7, 11), (2, 4, 8, 10), (0, 3, 6, 9))
OFFSETS = SETS[0] + SETS[1] + SETS[2]
LEN = len(SETS[0])
CHUNK = ROWS // len(SETS)
UNITS = tuple((kind, chunk) for kind in range(2) for chunk in range(len(SETS)))
STEPS = (("turn", 0.0), ("sum", 7.0), ("sum_x", 9.5), ("act", 14.0), ("forward", 18.5), ("out", 20.5), ("back", 28.5))
BETWEEN = 3.7


def spread(k, n):
    return n // 2 + (k // 2) * (1 - 2 * (k % 2))


def dot(a, b, contract_a=1, contract_b=0):
    return lax.dot_general(a, b, (((contract_a,), (contract_b,)), ((), ())), preferred_element_type=F32)


def each(n, step):
    for k in range(1, n):
        step(k)


def layer(
    tok_hbm, cot_hbm, slot_ref, weight_ref, gate_hbm, down_hbm,
    mixed_ref, grad_ref, gate_grad_hbm, down_grad_hbm,
    tok_src, cot_src, gate_w, down_w, pick, perm_out, perm_back,
    z_out, z_in, y_out, y_in, rows,
    core_out, core_in, own, x_out, x_in, hid, gate_keep,
    yb_out, yb_in, zb_out, zb_in, weight_grads,
    load_sem, store_sem,
    z_send, z_recv, y_send, y_recv, c_send, c_recv, x_send, x_recv,
    g_send, g_recv, f_send, f_recv, yb_send, yb_recv, zb_send, zb_recv,
):
    dp, ex = lax.axis_index("dp"), lax.axis_index("expert")
    y, z = dp // NZ, dp % NZ
    x, core = ex // NCORE, ex % NCORE
    other = 1 - core
    mats = (gate_w, down_w)

    def at_z(off):
        return (y * NZ + (z + off) % NZ, ex)

    def at_y(k):
        return (((y + spread(k, NY)) % NY) * NZ + z, ex)

    def at_x(k):
        return (dp, ((x + spread(k, NX)) % NX) * NCORE + core)

    at_core = (dp, x * NCORE + other)

    barrier = pltpu.get_barrier_semaphore()

    def hello(to):
        pl.semaphore_signal(barrier, inc=1, device_id=to, device_id_type=MESH)

    each(NZ, lambda k: hello(at_z(k)))
    each(NY, lambda k: hello(at_y(k)))
    each(NX, lambda k: hello(at_x(k)))
    hello(at_core)

    loads = [
        pltpu.make_async_copy(tok_hbm, tok_src.at[pl.ds(0, WIDTH), pl.ds(0, TOK)], load_sem.at[0]),
        pltpu.make_async_copy(tok_hbm, tok_src.at[pl.ds(WIDTH, WIDTH), pl.ds(TOK, TOK)], load_sem.at[1]),
        pltpu.make_async_copy(cot_hbm, cot_src.at[pl.ds(0, WIDTH), pl.ds(0, TOK)], load_sem.at[2]),
        pltpu.make_async_copy(cot_hbm, cot_src.at[pl.ds(WIDTH, WIDTH), pl.ds(TOK, TOK)], load_sem.at[3]),
        pltpu.make_async_copy(gate_hbm, gate_w.at[pl.ds(0, WIDTH)], load_sem.at[4]),
        pltpu.make_async_copy(down_hbm, down_w.at[pl.ds(0, WIDTH)], load_sem.at[5]),
    ]
    for load in loads:
        load.start()

    for src in (tok_src, cot_src):
        src[pl.ds(0, WIDTH), pl.ds(TOK, TOK)] = jnp.zeros((WIDTH, TOK), BF16)
        src[pl.ds(WIDTH, WIDTH), pl.ds(0, TOK)] = jnp.zeros((WIDTH, TOK), BF16)

    inner = lax.broadcasted_iota(jnp.int32, (2 * NY, TOK), 0)
    to = jnp.concatenate([(inner >> 1) * NZ + (z + off) % NZ for off in OFFSETS], axis=0)
    odd = (lax.broadcasted_iota(jnp.int32, (ROWS, TOK), 0) & 1) == 1
    half = NY * NZ // 2
    slot = jnp.where(odd, 2 * jnp.where(to < half, to + half, to - half) + 1, 2 * to)
    is_0, is_1 = slot == slot_ref[0:1, :], slot == slot_ref[1:2, :]
    named = jnp.where(is_0 | is_1, 1.0, 0.0)
    earlier = lax.broadcasted_iota(jnp.int32, (TOK, TOK), 0) < lax.broadcasted_iota(jnp.int32, (TOK, TOK), 1)
    before = dot(named.astype(BF16), jnp.where(earlier, 1.0, 0.0).astype(BF16))
    first = jnp.where(before < 0.5, 1.0, 0.0)
    later = 1.0 - first
    chosen = jnp.concatenate([named * first, named * later], axis=1).astype(BF16)
    loads[0].wait()
    loads[1].wait()
    z_out[0] = dot(chosen, tok_src[...], 1, 1).astype(BF16).reshape(NZ, 2 * NY, LANES)
    pl.semaphore_wait(barrier, NZ + NY + NX + NCORE - 4)

    def z_copy(src, dst, send, recv, kind, q):
        return pltpu.make_async_remote_copy(
            src_ref=src.at[kind, q], dst_ref=dst.at[kind, q], send_sem=send.at[kind, q], recv_sem=recv.at[kind, q],
            device_id=at_z(OFFSETS[q]), device_id_type=MESH)

    def zb_copy(src, dst, send, recv, kind, q):
        return pltpu.make_async_remote_copy(
            src_ref=src.at[kind, q], dst_ref=dst.at[kind, q], send_sem=send.at[kind, q], recv_sem=recv.at[kind, q],
            device_id=at_z(NZ - OFFSETS[q]), device_id_type=MESH)

    def y_copy(src, dst, send, recv, u, k):
        off = spread(k, NY)
        return pltpu.make_async_remote_copy(
            src_ref=src.at[u[0], u[1], (y + off) % NY], dst_ref=dst.at[u[0], u[1], y], send_sem=send.at[u[0], u[1], off],
            recv_sem=recv.at[u[0], u[1], off], device_id=at_y(k), device_id_type=MESH)

    def y_come(src, dst, send, recv, u, k):
        off = spread(k, NY)
        return pltpu.make_async_remote_copy(
            src_ref=src.at[u[0], u[1], y], dst_ref=dst.at[u[0], u[1], (y + NY - off) % NY], send_sem=send.at[u[0], u[1], off],
            recv_sem=recv.at[u[0], u[1], off], device_id=at_y(k), device_id_type=MESH)

    def part(u):
        return pl.ds(u[1] * CHUNK, CHUNK)

    def hid_rows(u, position):
        return pl.ds(pl.multiple_of(u[1] * 2 * CHUNK + position * CHUNK, CHUNK), CHUNK)

    def x_copy(u, k):
        off = spread(k, NX)
        return pltpu.make_async_remote_copy(
            src_ref=x_out.at[u[0], (x + off) % NX, part(u)], dst_ref=x_in.at[u[0], x, part(u)], send_sem=x_send.at[u[0], u[1], off],
            recv_sem=x_recv.at[u[0], u[1], off], device_id=at_x(k), device_id_type=MESH)

    def x_come(u, k):
        off = spread(k, NX)
        return pltpu.make_async_remote_copy(
            src_ref=x_out.at[u[0], x, part(u)], dst_ref=x_in.at[u[0], (x + NX - off) % NX, part(u)], send_sem=x_send.at[u[0], u[1], off],
            recv_sem=x_recv.at[u[0], u[1], off], device_id=at_x(k), device_id_type=MESH)

    def g_copy(u, k):
        off = spread(k, NX)
        mine = hid.at[u[0], x, hid_rows(u, core)]
        return pltpu.make_async_remote_copy(
            src_ref=mine, dst_ref=mine, send_sem=g_send.at[u[0], u[1], off],
            recv_sem=g_recv.at[u[0], u[1], off], device_id=at_x(k), device_id_type=MESH)

    def g_come(u, k):
        off = spread(k, NX)
        return pltpu.make_async_remote_copy(
            src_ref=hid.at[u[0], x, hid_rows(u, core)], dst_ref=hid.at[u[0], (x + NX - off) % NX, hid_rows(u, core)],
            send_sem=g_send.at[u[0], u[1], off], recv_sem=g_recv.at[u[0], u[1], off], device_id=at_x(k), device_id_type=MESH)

    def f_copy(u):
        block = hid.at[u[0], :, hid_rows(u, core)]
        return pltpu.make_async_remote_copy(
            src_ref=block, dst_ref=block, send_sem=f_send.at[u[0], u[1]],
            recv_sem=f_recv.at[u[0], u[1]], device_id=at_core, device_id_type=MESH)

    def f_come(u):
        return pltpu.make_async_remote_copy(
            src_ref=hid.at[u[0], :, hid_rows(u, core)], dst_ref=hid.at[u[0], :, hid_rows(u, other)],
            send_sem=f_send.at[u[0], u[1]], recv_sem=f_recv.at[u[0], u[1]], device_id=at_core, device_id_type=MESH)

    def c_copy(u):
        return pltpu.make_async_remote_copy(
            src_ref=core_out.at[u[0], part(u)], dst_ref=core_in.at[u[0], part(u)], send_sem=c_send.at[u[0], u[1]],
            recv_sem=c_recv.at[u[0], u[1]], device_id=at_core, device_id_type=MESH)

    blocks = [[q for q in range(c * LEN, (c + 1) * LEN)] for c in range(len(SETS))]
    far = (NX - 1, NX - 2, 1)

    def send_z(u):
        for q in blocks[u[1]]:
            if OFFSETS[q]:
                z_copy(z_out, z_in, z_send, z_recv, u[0], q).start()
            else:
                z_in[u[0], q] = z_out[u[0], q]

    def send_y(value, src, dst, send, recv, u):
        src[u[0], u[1]] = value.reshape(NY, 2 * LEN, LANES).astype(BF16)
        each(NY, lambda k: y_copy(src, dst, send, recv, u, k).start())
        dst[u[0], u[1], y] = src[u[0], u[1], y]

    def take_y(src, dst, send, recv, u):
        each(NY, lambda k: y_come(src, dst, send, recv, u, k).wait_recv())
        return dst[u[0], u[1]].astype(F32).reshape(CHUNK, LANES)

    def turn(u):
        for q in blocks[u[1]]:
            if OFFSETS[q]:
                z_copy(z_out, z_in, z_send, z_recv, u[0], q).wait_recv()
        got = z_in[u[0], pl.ds(u[1] * LEN, LEN)].reshape(CHUNK, LANES)
        send_y(dot(perm_out[...], got), y_out, y_in, y_send, y_recv, u)

    def partial_sum(u):
        got = take_y(y_out, y_in, y_send, y_recv, u)
        right = pltpu.roll(got[:, LANES - TILE:], WIDTH, 1)
        both = jnp.concatenate([got[:, :TILE], right], axis=0).astype(BF16)
        rows[u[0], pl.ds(u[1] * 2 * CHUNK, 2 * CHUNK)] = both
        total = dot(both, mats[u[0]][...])
        low, high = total[:CHUNK], total[CHUNK:]
        core_out[u[0], part(u)] = jnp.where(core == 0, high, low).astype(BF16)
        c_copy(u).start()
        own[u[0], part(u)] = jnp.where(core == 0, low, high)

    def sum_x(u):
        c_copy(u).wait_recv()
        total = own[u[0], part(u)] + core_in[u[0], part(u)].astype(F32)
        own[u[0], part(u)] = total
        for i in range(NX):
            x_out[u[0], i, part(u)] = total[:, i * COLS:(i + 1) * COLS].astype(BF16)
        each(NX, lambda k: x_copy(u, k).start())

    def act(u):
        each(NX, lambda k: x_come(u, k).wait_recv())
        total = own[u[0], part(u), pl.ds(pl.multiple_of(x * COLS, COLS), COLS)]
        for off in range(1, NX):
            total = total + x_in[u[0], (x + NX - off) % NX, part(u)].astype(F32)
        if u[0] == 0:
            gate_keep[part(u)] = total
            value = total * jax.nn.sigmoid(total)
        else:
            gate = gate_keep[part(u)]
            sig = jax.nn.sigmoid(gate)
            value = total * sig * (1.0 + gate * (1.0 - sig))
        hid[u[0], x, hid_rows(u, core)] = value.astype(BF16)
        each(NX, lambda k: g_copy(u, k).start())

    def forward(u):
        for k in far:
            g_come(u, k).wait_recv()
        f_copy(u).start()

    def out(u):
        f_come(u).wait_recv()
        both = pl.ds(u[1] * 2 * CHUNK, 2 * CHUNK)
        value = jnp.concatenate([hid[u[0], i, both] for i in range(NX)], axis=1)
        value = dot(value, mats[1 - u[0]][...], 1, 1)
        left, right = value[:CHUNK], pltpu.roll(value[CHUNK:], TILE - WIDTH, 1)
        cut = LANES - TILE
        value = jnp.concatenate([left[:, :cut], left[:, cut:] + right[:, :TILE - cut], right[:, TILE - cut:]], axis=1)
        send_y(value, yb_out, yb_in, yb_send, yb_recv, u)

    def back(u):
        got = take_y(yb_out, yb_in, yb_send, yb_recv, u).astype(BF16)
        zb_out[u[0], pl.ds(u[1] * LEN, LEN)] = dot(perm_back[...], got).astype(BF16).reshape(LEN, 2 * NY, LANES)
        for q in blocks[u[1]]:
            if OFFSETS[q]:
                zb_copy(zb_out, zb_in, zb_send, zb_recv, u[0], q).start()
            else:
                zb_in[u[0], q] = zb_out[u[0], q]

    def picked(kind, c, n):
        for q in range(c * LEN, (c + n) * LEN):
            if OFFSETS[q]:
                zb_copy(zb_out, zb_in, zb_send, zb_recv, kind, q).wait_recv()
        got = zb_in[kind, pl.ds(c * LEN, n * LEN)].reshape(n * CHUNK, LANES)
        here = pl.ds(c * CHUNK, n * CHUNK)
        left = dot(got[:, :TILE], pick[0, here], 0, 0)
        right = dot(got[:, LANES - TILE:], pick[1, here], 0, 0)
        return left[:WIDTH] + right[TILE - WIDTH:]

    stores = [
        pltpu.make_async_copy(weight_grads.at[kind], result, store_sem.at[kind])
        for kind, result in enumerate((gate_grad_hbm, down_grad_hbm))]

    def weight_grad(kind):
        for i in range(NX):
            grad = dot(rows[kind], hid[1 - kind, i], 0, 0)
            weight_grads[kind, :, pl.ds(i * COLS, COLS)] = grad[:WIDTH].astype(BF16)
        stores[kind].start()

    send_z(UNITS[0])
    send_z(UNITS[1])
    one_0, one_1 = jnp.where(is_0, 1.0, 0.0), jnp.where(is_1, 1.0, 0.0)
    weight_of = one_0 * weight_ref[0:1, :] + one_1 * weight_ref[1:2, :]
    scale_first = jnp.sum(weight_of * first, axis=1, keepdims=True)
    scale_later = jnp.sum(weight_of * later, axis=1, keepdims=True)
    lane = lax.broadcasted_iota(jnp.int32, (ROWS, LANES), 1)
    scale = jnp.where(lane < WIDTH, scale_first, scale_later)
    loads[2].wait()
    loads[3].wait()
    z_out[1] = (scale * dot(chosen, cot_src[...], 1, 1)).astype(BF16).reshape(NZ, 2 * NY, LANES)
    pick[0] = jnp.concatenate([one_0 * first, one_1 * first], axis=1).astype(BF16)
    pick[1] = jnp.concatenate([one_0 * later, one_1 * later], axis=1).astype(BF16)
    down_axis = lax.broadcasted_iota(jnp.int32, (CHUNK, CHUNK), 0)
    along_axis = lax.broadcasted_iota(jnp.int32, (CHUNK, CHUNK), 1)

    def place(c):
        return ((c >> 1) & (NY - 1)) * (2 * LEN) + (c >> 4) * 2 + (c & 1)

    perm_out[...] = jnp.where(down_axis == place(along_axis), 1.0, 0.0).astype(BF16)
    perm_back[...] = jnp.where(place(down_axis) == along_axis, 1.0, 0.0).astype(BF16)
    for mat in mats:
        mat[pl.ds(WIDTH, TILE - WIDTH), :] = jnp.zeros((TILE - WIDTH, HW), BF16)
    loads[4].wait()
    loads[5].wait()

    names = dict(turn=turn, sum=partial_sum, sum_x=sum_x, act=act, forward=forward, out=out, back=back)
    plan = sorted(
        ((n * BETWEEN + at, n, name) for n in range(len(UNITS)) for name, at in STEPS), key=lambda e: e[:2])
    for _, n, name in plan:
        names[name](UNITS[n])
        if name == "turn" and n + 2 < len(UNITS):
            send_z(UNITS[n + 2])
        if name == "out" and n == len(UNITS) - 1:
            weight_grad(1)
    weight_grad(0)
    both = picked(0, 0, len(SETS))
    mixed_ref[...] = (both[:, :TOK] * weight_ref[0:1, :] + both[:, TOK:] * weight_ref[1:2, :]).astype(BF16)
    both = picked(1, 0, len(SETS) - 1)
    both = both + picked(1, len(SETS) - 1, 1)
    grad_ref[...] = (both[:, :TOK] + both[:, TOK:]).astype(BF16)

    for u in UNITS:
        for q in blocks[u[1]]:
            if OFFSETS[q]:
                z_copy(z_out, z_in, z_send, z_recv, u[0], q).wait_send()
                zb_copy(zb_out, zb_in, zb_send, zb_recv, u[0], q).wait_send()
        each(NY, lambda k: y_copy(y_out, y_in, y_send, y_recv, u, k).wait_send())
        each(NY, lambda k: y_copy(yb_out, yb_in, yb_send, yb_recv, u, k).wait_send())
        each(NX, lambda k: x_copy(u, k).wait_send())
        each(NX, lambda k: g_copy(u, k).wait_send())
        f_copy(u).wait_send()
        c_copy(u).wait_send()
    for store in stores:
        store.wait()


def write(*refs):
    n = len(refs) // 2
    copies = [pltpu.make_async_copy(refs[i], refs[n + i], refs[2 * n].at[i]) for i in range(n)]
    for copy in copies:
        copy.start()
    for copy in copies:
        copy.wait()


def per_device(tokens, cotangent, slot_route, route_weight, w_gate, w_down):
    hbm, vmem = pl.BlockSpec(memory_space=pltpu.HBM), pl.BlockSpec(memory_space=pltpu.VMEM)
    dma = pltpu.SemaphoreType.DMA
    chunks = len(SETS)
    shapes = (
        jax.ShapeDtypeStruct((WIDTH, TOK), BF16),
        jax.ShapeDtypeStruct((WIDTH, TOK), BF16),
        jax.ShapeDtypeStruct((WIDTH, HW), BF16),
        jax.ShapeDtypeStruct((WIDTH, HW), BF16),
    )
    results = pl.pallas_call(
        layer,
        out_shape=shapes,
        in_specs=[hbm, hbm, vmem, vmem, hbm, hbm],
        out_specs=(vmem, vmem, hbm, hbm),
        scratch_shapes=[
            pltpu.VMEM((LANES, 2 * TOK), BF16), pltpu.VMEM((LANES, 2 * TOK), BF16),
            pltpu.VMEM((TILE, HW), BF16), pltpu.VMEM((TILE, HW), BF16),
            pltpu.VMEM((2, ROWS, 2 * TOK), BF16),
            pltpu.VMEM((CHUNK, CHUNK), BF16), pltpu.VMEM((CHUNK, CHUNK), BF16),
            pltpu.VMEM((2, NZ, 2 * NY, LANES), BF16), pltpu.VMEM((2, NZ, 2 * NY, LANES), BF16),
            pltpu.VMEM((2, chunks, NY, 2 * LEN, LANES), BF16), pltpu.VMEM((2, chunks, NY, 2 * LEN, LANES), BF16),
            pltpu.VMEM((2, 2 * ROWS, TILE), BF16),
            pltpu.VMEM((2, ROWS, HW), BF16), pltpu.VMEM((2, ROWS, HW), BF16),
            pltpu.VMEM((2, ROWS, HW), F32),
            pltpu.VMEM((2, NX, ROWS, COLS), BF16), pltpu.VMEM((2, NX, ROWS, COLS), BF16),
            pltpu.VMEM((2, NX, 2 * ROWS, COLS), BF16),
            pltpu.VMEM((ROWS, COLS), F32),
            pltpu.VMEM((2, chunks, NY, 2 * LEN, LANES), BF16), pltpu.VMEM((2, chunks, NY, 2 * LEN, LANES), BF16),
            pltpu.VMEM((2, NZ, 2 * NY, LANES), BF16), pltpu.VMEM((2, NZ, 2 * NY, LANES), BF16),
            pltpu.VMEM((2, WIDTH, HW), BF16),
            dma((6,)), dma((2,)),
            dma((2, NZ)), dma((2, NZ)), dma((2, chunks, NY)), dma((2, chunks, NY)), dma((2, chunks)), dma((2, chunks)),
            dma((2, chunks, NX)), dma((2, chunks, NX)), dma((2, chunks, NX)), dma((2, chunks, NX)),
            dma((2, chunks)), dma((2, chunks)),
            dma((2, chunks, NY)), dma((2, chunks, NY)), dma((2, NZ)), dma((2, NZ)),
        ],
        compiler_params=pltpu.CompilerParams(
            collective_id=0, has_side_effects=True, vmem_limit_bytes=58 * 1024 * 1024),
        name="moe_layer",
    )(tokens.T, cotangent.T, slot_route.T, route_weight.T, w_gate[0], w_down[0].T)
    mixed, input_grad, gate_grad, down_grad = pl.pallas_call(
        write,
        out_shape=shapes,
        in_specs=[vmem] * 4,
        out_specs=(hbm,) * 4,
        scratch_shapes=[dma((4,))],
        name="write_results",
    )(*results)
    return mixed.T, input_grad.T, gate_grad[None], down_grad.T[None]


def solution(mesh):
    return jax.shard_map(
        per_device,
        mesh=mesh,
        in_specs=(
            P("dp", "expert"),
            P("dp", "expert"),
            P("dp", None),
            P("dp", None),
            P("dp", "expert", None),
            P("dp", None, "expert"),
        ),
        out_specs=(
            P("dp", "expert"),
            P("dp", "expert"),
            P("dp", "expert", None),
            P("dp", None, "expert"),
        ),
        check_vma=False,
    )
```
